32 devices in a mesh: groups: 2 (over y), expert: 8 (over z, core), section: 2 (over x).
Axes of the slice: x: 2, y: 2, z: 4, core: 2. Of those that a mesh axis runs over, the one named last changes fastest.
Arguments:
- activations: bfloat16 [2, 64, 128, 6144], P('section', 'groups', 'expert'), parts along dimension 1, may hold values from -6 to 6
- block_expert: int32 [2, 64, 1], P('section', 'groups'), parts along dimension 1, may hold values from 0 to 7; in each aligned block of 32 rows (0 to 31, 32 to 63, ..., all dimensions but the last counted through in order) at most 8 rows name the same one
- seq_task: int32 [2, 16], P('section', 'groups'), parts along dimension 1, may hold values from 0 to 7
- norm_gain: bfloat16 [2, 6144], P('section'), may hold values from 0.099609375 to 1.8984375
- task_embed: bfloat16 [8, 256], replicated, may hold values from -6 to 6
- expert_embed: bfloat16 [2, 8, 256], P('section'), may hold values from -6 to 6
- gen_down: bfloat16 [2, 256, 16, 6144], P('section', None, None, 'expert'), may hold values from -0.0048828125 to 0.0048828125
- gen_up: bfloat16 [2, 256, 16, 6144], P('section', None, None, 'expert'), may hold values from -0.09375 to 0.09375
Outputs:
- handoff: bfloat16 [2, 64, 128, 6144], P('section', 'groups', 'expert'), parts along dimension 1
The draws below stay inside these ranges and needn't reach their ends.
There are 2 independent parts, one for each index of `groups`. The reference program is written for one: setup_inputs(seed, part) draws one part's arguments, and reference() takes and returns one part's arrays. A program takes and returns all parts, laid end to end along the dimension named above; an argument that names none is the same for every part. Nothing has to cross between parts.
Inputs may be any that keep to these rules, and one draw needn't show every extreme that they name: `block_expert`: within each layer's 32 blocks no expert is named more than 8 times, and one expert exactly 8 times.
All inputs are finite; a program needn't handle non-finite values.
Results may differ from the reference program's by a relative error of at most 0.0065.
Values may be sent and summed in bfloat16 or wider, within the bound.
No kernel may reach another device: no remote copies, remote signals or barrier semaphores. Data moves between devices by JAX's collectives and lax.ppermute only.
A program may use at most 192 MiB of HBM per device.

```python
import math
import jax
import jax.numpy as jnp
import numpy as np
from jax import lax

D = 6144
EXPERTS = 8
R = 16
HYP = 256
BLOCK_ROWS = 128
SEQ_BLOCKS = 4
TASKS = 8
BLOCKS = 32
MOST = 8
SEQS = 8
LAYERS = 2


def with_ends(entries, rng, smallest, largest):
    longest = entries.shape.index(max(entries.shape))
    spots = []
    for shift in (0, 1):
        where = [jax.random.randint(jax.random.fold_in(rng, axis), (), 0, length) for axis, length in enumerate(entries.shape)]
        where[longest] = (where[longest] + shift) % entries.shape[longest]
        spots.append(tuple(where))
    return entries.at[spots[0]].set(smallest).at[spots[1]].set(largest)


def levels(stream_key, shape, pieces, smallest, top_value):
    def one(axis_at, shards_of):
        steps = jax.random.uniform(jax.random.fold_in(jax.random.fold_in(stream_key, 6), axis_at), (shards_of,), jnp.float32, smallest / len(pieces), top_value / len(pieces))
        return jnp.repeat(jnp.exp(steps), shape[axis_at] // shards_of).reshape((-1,) + (1,) * (len(shape) - axis_at - 1))

    gain = one(*pieces[0])
    for cut in pieces[1:]:
        gain = gain * one(*cut)
    return gain


def deal_out(key, own, number, rows, amount, top, bound, lean):
    sequence = jax.random.permutation(key, amount)
    crowded, usual = shares(amount, rows * top, bound, lean, True), shares(amount, rows * top, bound, lean, False)
    places = jnp.arange(amount)

    def named(sizes, rotation):
        used = int((sizes > 0).sum())
        fixed = max(1, used // 4)
        moved = fixed + (places - fixed + rotation * (used - fixed)) % max(1, amount - fixed)
        return jnp.zeros((amount,), jnp.int32).at[sequence[jnp.where(places < fixed, places, moved)]].set(jnp.asarray(sizes, jnp.int32))

    sizes = jnp.where(number % 4 == 0, named(crowded, number // 4), named(usual, number - number // 4 - 1))
    mixed = jax.random.permutation(jax.random.fold_in(own, 3), amount)
    source_of, receiver = mixed[0:amount // 2 * 2:2], mixed[1:amount // 2 * 2:2]
    slack = jnp.minimum(sizes[source_of] - 1, bound - sizes[receiver]) // 2
    slack = jnp.where((source_of == sequence[0]) | (receiver == sequence[0]) | (sizes[receiver] == 0), 0, jnp.maximum(slack, 0))
    moved = jax.random.randint(jax.random.fold_in(own, 4), (amount // 2,), 0, 1 << 20) % (slack + 1)
    sizes = sizes.at[source_of].add(-moved).at[receiver].add(moved)
    labels = jnp.searchsorted(jnp.cumsum(sizes), jnp.arange(rows * top), side="right").astype(jnp.int32)
    grid = labels.reshape(top, rows).T
    grid = grid[jax.random.permutation(jax.random.fold_in(own, 1), rows)]
    rotation = jax.random.randint(jax.random.fold_in(own, 2), (rows, 1), 0, top)
    return jnp.take_along_axis(grid, (jnp.arange(top)[None, :] + rotation) % top, axis=1)


def shares(amount, total, limit, slope, full):
    loads = [(1 << 20) // math.isqrt(rank ** slope) + 1 for rank in range(1, amount + 1)]
    largest = limit if full else min(limit, max(-(-total // amount), total * loads[0] // sum(loads)))
    least = 1 if total - largest >= amount - 1 else 0
    given, spare = [largest] + [least] * (amount - 1), total - largest - least * (amount - 1)
    while spare > 0:
        candidates = [i for i in range(1, amount) if given[i] < largest] or [i for i in range(1, amount) if given[i] < limit]
        whole, remaining = sum([loads[i] for i in candidates]), spare
        for i in candidates:
            extra = min(limit - given[i], max(1, remaining * loads[i] // whole), spare)
            given[i] = given[i] + extra
            spare = spare - extra
    return np.array(given)


def noise(stream_key, dims, width, reach, cuts=(), kind=jnp.bfloat16):
    result = width * jax.random.normal(stream_key, dims, jnp.float32)
    if cuts:
        result = result * levels(stream_key, dims, cuts, -0.22, 0.18)
    return jnp.clip(result, -reach, reach).astype(kind)


def setup_inputs(seed: int = 0, part: int = 0) -> dict:
    streams_of = jax.random.split(jax.random.key(seed), 9)
    part_keys = jax.random.split(jax.random.fold_in(streams_of[8], part), 9)
    activations = noise(part_keys[0], (LAYERS, BLOCKS, BLOCK_ROWS, D), 1.0, 6.0, ((0, 2), (2, 8)))
    block_expert_keys = jax.random.split(jax.random.fold_in(part_keys[1], 1), LAYERS * BLOCKS // BLOCKS)
    block_expert_turns = jax.random.permutation(jax.random.fold_in(part_keys[1], 3), LAYERS * BLOCKS // BLOCKS)
    block_expert = jax.vmap(lambda own, number: deal_out(jax.random.fold_in(part_keys[1], 2), own, number, BLOCKS, EXPERTS, 1, MOST, 2))(block_expert_keys, block_expert_turns).reshape((LAYERS, BLOCKS, 1))
    seq_task = with_ends(jax.random.randint(part_keys[2], (LAYERS, SEQS), 0, TASKS), jax.random.fold_in(part_keys[2], 1), 0, TASKS - 1).astype(jnp.int32)
    norm_gain = jnp.clip(1.0 + 0.18 * jax.random.normal(streams_of[3], (LAYERS, D), jnp.float32), 0.099609375, 1.8984375).astype(jnp.bfloat16)
    task_embed = noise(streams_of[4], (TASKS, HYP), 1.0, 6.0)
    expert_embed = noise(streams_of[5], (LAYERS, EXPERTS, HYP), 1.0, 6.0, ((0, 2),))
    gen_down = noise(streams_of[6], (LAYERS, HYP, R, D), (HYP * D) ** -0.5, 0.0048828125, ((0, 2), (3, 8)))
    gen_up = noise(streams_of[7], (LAYERS, HYP, R, D), (HYP * R) ** -0.5, 0.09375, ((0, 2), (3, 8)))
    return dict(activations=activations, block_expert=block_expert, seq_task=seq_task, norm_gain=norm_gain, task_embed=task_embed, expert_embed=expert_embed, gen_down=gen_down, gen_up=gen_up)


def section_layer(activations, block_expert, seq_task, norm_gain, task_embed, expert_embed, gen_down, gen_up):
    code = jax.nn.silu(task_embed.astype(jnp.float32)[:, None, :] + expert_embed.astype(jnp.float32)[None]).astype(jnp.bfloat16)
    down_all = jnp.einsum('keh,hrd->kerd', code.astype(jnp.float32), gen_down.astype(jnp.float32)).astype(jnp.bfloat16)
    up_all = jnp.einsum('keh,hrd->kerd', code.astype(jnp.float32), gen_up.astype(jnp.float32)).astype(jnp.bfloat16)
    expert_ids = block_expert[:, 0].astype(jnp.int32)
    task_ids = seq_task[jnp.arange(BLOCKS, dtype=jnp.int32) // SEQ_BLOCKS].astype(jnp.int32)
    down_rows = down_all[task_ids, expert_ids]
    up_rows = up_all[task_ids, expert_ids]
    values = activations.astype(jnp.float32)
    scale = lax.rsqrt(lax.optimization_barrier(jnp.mean(values * values, axis=-1, keepdims=True)) + 1e-05)
    normed = (values * scale * norm_gain.astype(jnp.float32)).astype(jnp.bfloat16)
    low = jnp.einsum('bnd,brd->bnr', normed.astype(jnp.float32), down_rows.astype(jnp.float32)).astype(jnp.bfloat16)
    update = jnp.einsum('bnr,brd->bnd', low.astype(jnp.float32), up_rows.astype(jnp.float32))
    return (values + update).astype(jnp.bfloat16)

def reference(activations, block_expert, seq_task, norm_gain, task_embed, expert_embed, gen_down, gen_up):
    results = []
    for section in range(LAYERS):
        results.append(section_layer(activations[section], block_expert[section], seq_task[section], norm_gain[section], task_embed, expert_embed[section], gen_down[section], gen_up[section]))
    return jnp.stack(results[-1:] + results[:-1])
```

```python
import functools

import jax
import jax.numpy as jnp
from jax import lax
from jax.experimental import pallas as pl
from jax.experimental.pallas import tpu as pltpu
from jax.sharding import PartitionSpec as P

CORES = 2
VMEM_BYTES = 40 * 1024 * 1024


def passed_along(block, axis, distance):
    devices = range(lax.axis_size(axis))
    route = [((i - distance) % len(devices), i) for i in devices]
    return lax.ppermute(block, axis, route)


def chip_ring(n_chips):
    return list(range(0, n_chips, 2)) + list(range(1, n_chips, 2))[::-1]


def ring_step(block):
    order = chip_ring(lax.axis_size("expert") // CORES)
    route = []
    for at, chip in enumerate(order):
        after = order[(at + 1) % len(order)]
        route += [(chip * CORES + core, after * CORES + core) for core in range(CORES)]
    return lax.ppermute(block, "expert", route)


def core_swap(block):
    route = [(i, i ^ 1) for i in range(lax.axis_size("expert"))]
    return lax.ppermute(block, "expert", route)


def piece_owners(n_devices):
    order = chip_ring(n_devices // CORES)
    owners = []
    for device in range(n_devices):
        chip, core = divmod(device, CORES)
        at = order.index(chip)
        row = []
        for step in range(len(order)):
            source = order[(at - step) % len(order)]
            row += [source * CORES + core, source * CORES + 1 - core]
        owners.append(row)
    return jnp.asarray(owners, jnp.int32)


def tied(value, *after):
    return lax.optimization_barrier((value, *after))[0]


def ring_gather(block):
    pieces, held = [], block
    for step in range(lax.axis_size("expert") // CORES):
        if step:
            held = ring_step(held)
        pieces += [held, core_swap(held)]
    return pieces


def columns(owners_ref, piece, width):
    return pl.ds(pl.multiple_of(owners_ref[piece] * width, 128), width)


def normed_into(normed_ref, rows_ref, gain_ref):
    values = rows_ref[0].astype(jnp.float32)
    scale = lax.rsqrt(jnp.mean(values * values, axis=-1, keepdims=True) + 1e-05)
    normed_ref[...] = (values * scale * gain_ref[...].astype(jnp.float32)).astype(jnp.bfloat16)


def low_of(owners_ref, normed_ref, maps, width):
    total = None
    for piece, down in enumerate(maps):
        part = lax.dot_general(
            normed_ref[:, columns(owners_ref, piece, width)],
            down,
            (((1,), (1,)), ((), ())),
            preferred_element_type=jnp.float32,
        )
        total = part if total is None else total + part
    return total.astype(jnp.bfloat16)


def add_update(owners_ref, out_ref, rows_ref, low, maps, width):
    for piece, up in enumerate(maps):
        at = columns(owners_ref, piece, width)
        update = jnp.dot(low, up, preferred_element_type=jnp.float32)
        out_ref[0, :, at] = (rows_ref[0, :, at].astype(jnp.float32) + update).astype(jnp.bfloat16)


def layer_kernel(n, width, owners_ref, rows_ref, gain_ref, *refs):
    pieces, out_ref, normed_ref = refs[:n], refs[n], refs[n + 1]
    normed_into(normed_ref, rows_ref, gain_ref)
    low = low_of(owners_ref, normed_ref, [p[0, 0] for p in pieces], width)
    add_update(owners_ref, out_ref, rows_ref, low, [p[1, 0] for p in pieces], width)


def low_kernel(n, width, owners_ref, rows_ref, gain_ref, *refs):
    pieces, out_ref, normed_ref = refs[:n], refs[n], refs[n + 1]
    normed_into(normed_ref, rows_ref, gain_ref)
    out_ref[0] = low_of(owners_ref, normed_ref, [p[0] for p in pieces], width)


def update_kernel(n, width, owners_ref, rows_ref, low_ref, *refs):
    pieces, out_ref = refs[:n], refs[-1]
    add_update(owners_ref, out_ref, rows_ref, low_ref[0], [p[0] for p in pieces], width)


def place_kernel(block_ref, held_ref, out_ref):
    out_ref[...] = block_ref[...]


def params():
    return pltpu.CompilerParams(vmem_limit_bytes=VMEM_BYTES)


def cost(count, rows, dim, rank, passes):
    return pl.CostEstimate(
        flops=4 * count * rows * dim * rank,
        bytes_accessed=2 * count * dim * (passes * rows + 2 * rank),
        transcendentals=0,
    )


def layer_blocks(owners, rows, first, gain, pieces):
    n, (_, count, rank, width) = len(pieces), pieces[0].shape
    held, dim = rows.shape[1:]
    return pl.pallas_call(
        functools.partial(layer_kernel, n, width),
        out_shape=jax.ShapeDtypeStruct((count, held, dim), jnp.bfloat16),
        grid_spec=pltpu.PrefetchScalarGridSpec(
            num_scalar_prefetch=1,
            grid=(count,),
            in_specs=[
                pl.BlockSpec((1, held, dim), lambda b, s: (b + first, 0, 0)),
                pl.BlockSpec((1, dim), lambda b, s: (0, 0)),
            ]
            + [pl.BlockSpec((2, 1, rank, width), lambda b, s: (0, b, 0, 0))] * n,
            out_specs=pl.BlockSpec((1, held, dim), lambda b, s: (b, 0, 0)),
            scratch_shapes=[pltpu.VMEM((held, dim), jnp.bfloat16)],
        ),
        compiler_params=params(),
        cost_estimate=cost(count, held, dim, rank, 2),
    )(owners, rows, gain, *pieces)


def low_blocks(owners, rows, gain, pieces):
    n, (count, rank, width) = len(pieces), pieces[0].shape
    held, dim = rows.shape[1:]
    return pl.pallas_call(
        functools.partial(low_kernel, n, width),
        out_shape=jax.ShapeDtypeStruct((count, held, rank), jnp.bfloat16),
        grid_spec=pltpu.PrefetchScalarGridSpec(
            num_scalar_prefetch=1,
            grid=(count,),
            in_specs=[
                pl.BlockSpec((1, held, dim), lambda b, s: (b, 0, 0)),
                pl.BlockSpec((1, dim), lambda b, s: (0, 0)),
            ]
            + [pl.BlockSpec((1, rank, width), lambda b, s: (b, 0, 0))] * n,
            out_specs=pl.BlockSpec((1, held, rank), lambda b, s: (b, 0, 0)),
            scratch_shapes=[pltpu.VMEM((held, dim), jnp.bfloat16)],
        ),
        compiler_params=params(),
        cost_estimate=cost(count, held, dim, rank, 1),
    )(owners, rows, gain, *pieces)


def update_blocks(owners, rows, low, pieces, result):
    n, (count, rank, width) = len(pieces), pieces[0].shape
    held, dim = rows.shape[1:]
    return pl.pallas_call(
        functools.partial(update_kernel, n, width),
        out_shape=jax.ShapeDtypeStruct(result.shape, result.dtype),
        grid_spec=pltpu.PrefetchScalarGridSpec(
            num_scalar_prefetch=1,
            grid=(count,),
            in_specs=[
                pl.BlockSpec((1, held, dim), lambda b, s: (b, 0, 0)),
                pl.BlockSpec((1, held, rank), lambda b, s: (b, 0, 0)),
            ]
            + [pl.BlockSpec((1, rank, width), lambda b, s: (b, 0, 0))] * n
            + [pl.BlockSpec(memory_space=pl.ANY)],
            out_specs=pl.BlockSpec((1, held, dim), lambda b, s: (b, 0, 0)),
        ),
        input_output_aliases={3 + n: 0},
        compiler_params=params(),
        cost_estimate=cost(count, held, dim, rank, 2),
    )(owners, rows, low, *pieces, result)


def place_blocks(block, first, result, total):
    count, held, dim = block.shape
    spec = pl.BlockSpec((1, held, dim), lambda b: (b, 0, 0))
    kernel = place_kernel if result is not None else (lambda b, o: place_kernel(b, None, o))
    return pl.pallas_call(
        kernel,
        out_shape=jax.ShapeDtypeStruct((total, held, dim), jnp.bfloat16),
        grid=(count,),
        in_specs=[spec] + ([pl.BlockSpec(memory_space=pl.ANY)] if result is not None else []),
        out_specs=pl.BlockSpec((1, held, dim), lambda b: (b + first, 0, 0)),
        input_output_aliases={1: 0} if result is not None else {},
        compiler_params=params(),
        cost_estimate=cost(count, held, dim, 0, 2),
    )(block, *([] if result is None else [result]))


def norm_rows(block_rows, gain):
    values = block_rows.astype(jnp.float32)
    scale = lax.rsqrt(jnp.mean(values * values, axis=-1, keepdims=True) + 1e-05)
    return (values * scale * gain.astype(jnp.float32)).astype(jnp.bfloat16)


def apply_adapter(block_rows, gain, down_maps, up_maps):
    values = block_rows.astype(jnp.float32)
    normed = norm_rows(block_rows, gain)
    low = jnp.einsum("bnd,brd->bnr", normed, down_maps, preferred_element_type=jnp.float32).astype(
        jnp.bfloat16
    )
    update = jnp.einsum("bnr,brd->bnd", low, up_maps, preferred_element_type=jnp.float32)
    return (values + update).astype(jnp.bfloat16)


def cuts(n_blocks):
    raw = n_blocks * 3 // 8
    sizes = [n_blocks // 8]
    while raw + sum(sizes) < n_blocks:
        left = n_blocks - raw - sum(sizes)
        sizes.append(left if left <= n_blocks // 5 else -(-left // -(-left // (n_blocks // 5))))
    starts = [raw + sum(sizes[:i]) for i in range(len(sizes))]
    return raw, [(a, a + s) for a, s in zip(starts, sizes)]


def on_device(
    activations, block_expert, seq_task, norm_gain, task_embed, expert_embed, gen_down, gen_up
):
    rows = activations[0]
    n_blocks = rows.shape[0]
    raw, chunks = cuts(n_blocks)
    tiled = rows.shape[1] % 16 == 0 and gen_down.shape[3] % 128 == 0 and raw > 0

    if tiled:
        raw_rows = passed_along(rows[:raw], "section", 1)

    expert_ids = block_expert[0, :, 0]
    per_seq = n_blocks // seq_task.shape[1]
    task_ids = seq_task[0][jnp.arange(n_blocks, dtype=jnp.int32) // per_seq]
    code_all = jax.nn.silu(
        task_embed.astype(jnp.float32)[:, None, :] + expert_embed[0].astype(jnp.float32)[None]
    ).astype(jnp.bfloat16)
    code_rows = code_all[task_ids, expert_ids]
    down_part = jnp.einsum(
        "bh,hrd->brd", code_rows, gen_down[0], preferred_element_type=jnp.float32
    ).astype(jnp.bfloat16)
    up_part = jnp.einsum(
        "bh,hrd->brd", code_rows, gen_up[0], preferred_element_type=jnp.float32
    ).astype(jnp.bfloat16)

    if not tiled:
        down_full, up_full = (
            lax.all_gather(down_part, "expert", axis=2, tiled=True),
            lax.all_gather(up_part, "expert", axis=2, tiled=True),
        )
        result = apply_adapter(rows, norm_gain[0], down_full, up_full)
        return passed_along(result[None], "section", 1)

    owners = piece_owners(lax.axis_size("expert"))[lax.axis_index("expert")]
    raw_up = passed_along(tied(up_part[:raw], down_part), "section", 1)
    raw_down = ring_gather(down_part[:raw])
    raw_low = passed_along(low_blocks(owners, rows, norm_gain, raw_down), "section", 1)

    gathered = [raw_down]
    arrived = []
    for first, last in chunks:
        mine = jnp.stack([down_part[first:last], up_part[first:last]])
        if len(gathered) > 1:
            mine = tied(mine, gathered[-2][-2])
        gathered.append(ring_gather(mine))
        done = layer_blocks(owners, rows, first, norm_gain, gathered[-1])
        arrived.append(passed_along(done, "section", 1))
    raw_ups = ring_gather(tied(raw_up, gathered[-2][-2]))

    result = None
    for (first, last), block in zip(chunks[:-1], arrived[:-1]):
        result = place_blocks(block, first, result, n_blocks)
    result = update_blocks(owners, raw_rows, raw_low, raw_ups, result)
    result = place_blocks(arrived[-1], chunks[-1][0], result, n_blocks)
    return result[None]


def solution(mesh):
    in_specs = (
        P("section", "groups", "expert", None),
        P("section", "groups", None),
        P("section", "groups"),
        P("section", None),
        P(),
        P("section", None, None),
        P("section", None, None, "expert"),
        P("section", None, None, "expert"),
    )
    out_specs = P("section", "groups", "expert", None)
    return jax.shard_map(
        on_device, mesh=mesh, in_specs=in_specs, out_specs=out_specs, check_vma=False
    )
```

```python
import functools
import math

import jax
import jax.numpy as jnp
from jax import lax
from jax.experimental import pallas as pl
from jax.experimental.pallas import tpu as pltpu
from jax.sharding import PartitionSpec as P

CORES = 2
LANES = 128
MIB = 1024 * 1024


def passed_along(block, axis, distance):
    devices = range(lax.axis_size(axis))
    route = [((i - distance) % len(devices), i) for i in devices]
    return lax.ppermute(block, axis, route)


def chip_ring(n_chips):
    return list(range(0, n_chips, 2)) + list(range(1, n_chips, 2))[::-1]


def ring_step(block):
    order = chip_ring(lax.axis_size("expert") // CORES)
    route = []
    for at, chip in enumerate(order):
        after = order[(at + 1) % len(order)]
        route += [(chip * CORES + core, after * CORES + core) for core in range(CORES)]
    return lax.ppermute(block, "expert", route)


def core_swap(block):
    route = [(i, i ^ 1) for i in range(lax.axis_size("expert"))]
    return lax.ppermute(block, "expert", route)


def piece_owner(me, piece, n_chips):
    chip, core = me // CORES, me % CORES
    at = jnp.where(chip % 2 == 0, chip // 2, n_chips - 1 - chip // 2)
    at = (at - piece // CORES + n_chips) % n_chips
    source = jnp.where(at < (n_chips + 1) // 2, 2 * at, 2 * (n_chips - 1 - at) + 1)
    return source * CORES + (core + piece) % CORES


def tied(value, *after):
    return lax.optimization_barrier((value, *after))[0]


def rows_and_columns(shape):
    return (lax.broadcasted_iota(jnp.int32, shape, axis) for axis in (0, 1))


def zero_one(condition):
    return jnp.where(condition, 1.0, 0.0).astype(jnp.bfloat16)


def dot(a, b, contract_b=0):
    return lax.dot_general(
        a, b, (((1,), (contract_b,)), ((), ())), preferred_element_type=jnp.float32
    )


def generator_kernel(
    chunks, rank, expert_ref, task_ref, task_embed_ref, expert_embed_ref, down_ref, up_ref, rows_ref, *refs
):
    whole_ref, raw_down_ref, carrier_ref = refs[:3]
    chunk_refs = refs[3 : 3 + len(chunks)]
    code_ref, tasks_ref, experts_ref, spread_ref, down_sum, up_sum, copied = refs[3 + len(chunks) :]
    step = pl.program_id(0)
    n_blocks, per_step = code_ref.shape[0], spread_ref.shape[2]
    per_seq = n_blocks // task_ref.shape[0]
    n_rows = n_blocks * rank
    width = down_ref.shape[3]
    raw = raw_down_ref.shape[0]
    pieces = carrier_ref.shape[2] // width
    carried = carrier_ref.shape[0] - raw // pieces
    copy = pltpu.make_async_copy(
        rows_ref.at[pl.ds(0, carried)], carrier_ref.at[pl.ds(0, carried)], copied
    )

    @pl.when(step == 0)
    def _():
        copy.start()
        tasks_ref[...] = task_embed_ref[...].astype(jnp.float32)
        experts_ref[...] = expert_embed_ref[0].astype(jnp.float32)
        for block in range(n_blocks):
            task = tasks_ref[pl.ds(task_ref[block // per_seq], 1), :]
            expert = experts_ref[pl.ds(expert_ref[block], 1), :]
            code_ref[pl.ds(block, 1), :] = task + expert
        code = jax.nn.silu(code_ref[...]).astype(jnp.bfloat16)
        row, block = rows_and_columns((n_rows, n_blocks))
        repeat = zero_one(row // rank == block)
        for part in range(spread_ref.shape[0]):
            columns = code[:, part * per_step : (part + 1) * per_step]
            spread_ref[part] = dot(repeat, columns).astype(jnp.bfloat16)
        down_sum[...] = jnp.zeros_like(down_sum)
        up_sum[...] = jnp.zeros_like(up_sum)

    entry, column = rows_and_columns((per_step, per_step * rank))
    wide = dot(spread_ref[step], zero_one(column // rank == entry)).astype(jnp.bfloat16)
    row, column = rows_and_columns(wide.shape)
    wide = jnp.where(row % rank == column % rank, wide, jnp.zeros_like(wide))
    down_sum[...] += dot(wide, down_ref[0].reshape(per_step * rank, width))
    up_sum[...] += dot(wide, up_ref[0].reshape(per_step * rank, width))

    @pl.when(step == pl.num_programs(0) - 1)
    def _():
        shape = (n_blocks, rank, width)
        down = down_sum[...].astype(jnp.bfloat16).reshape(shape)
        up = up_sum[...].astype(jnp.bfloat16).reshape(shape)
        whole_ref[0], whole_ref[1] = down, up
        raw_down_ref[...] = down[:raw]
        for (first, last), ref in zip(chunks, chunk_refs):
            ref[0], ref[1] = down[first:last], up[first:last]
        for block in range(raw):
            at = pl.ds(block % pieces * width, width)
            carrier_ref[carried + block // pieces, :, at] = up[block]
        copy.wait()


def generated(expert_ids, task_ids, task_embed, expert_embed, gen_down, gen_up, rows, raw, carried, chunks):
    _, hyp, rank, width = gen_down.shape
    n_blocks, held, dim = rows.shape
    per_step = math.gcd(hyp, 64)
    n_rows = n_blocks * rank
    shapes = [(2, n_blocks, rank, width), (raw, rank, width), (carried + raw * width // dim, held, dim)]
    shapes += [(2, last - first, rank, width) for first, last in chunks]

    def whole(shape):
        return pl.BlockSpec(shape, lambda h, *_: (0,) * len(shape))

    generator = pl.BlockSpec((1, per_step, rank, width), lambda h, *_: (0, h, 0, 0))
    return pl.pallas_call(
        functools.partial(generator_kernel, chunks, rank),
        out_shape=[jax.ShapeDtypeStruct(shape, jnp.bfloat16) for shape in shapes],
        grid_spec=pltpu.PrefetchScalarGridSpec(
            num_scalar_prefetch=2,
            grid=(hyp // per_step,),
            in_specs=[
                whole(task_embed.shape),
                whole(expert_embed.shape),
                generator,
                generator,
                pl.BlockSpec(memory_space=pl.ANY),
            ],
            out_specs=[whole(shape) for shape in shapes],
            scratch_shapes=[
                pltpu.VMEM((n_blocks, hyp), jnp.float32),
                pltpu.VMEM(task_embed.shape, jnp.float32),
                pltpu.VMEM(expert_embed.shape[1:], jnp.float32),
                pltpu.VMEM((hyp // per_step, n_rows, per_step), jnp.bfloat16),
                pltpu.VMEM((n_rows, width), jnp.float32),
                pltpu.VMEM((n_rows, width), jnp.float32),
                pltpu.SemaphoreType.DMA,
            ],
        ),
        compiler_params=params(),
        cost_estimate=tiny_cost(),
    )(expert_ids, task_ids, task_embed, expert_embed, gen_down, gen_up, rows)


def columns(me_ref, piece, n_pieces, width):
    owner = piece_owner(me_ref[0], piece, n_pieces // CORES)
    return pl.ds(pl.multiple_of(owner * width, 128), width)


def flat(block):
    return block.reshape(-1, block.shape[-1])


def own_blocks(matrix, rank):
    row, column = rows_and_columns(matrix.shape)
    n_rows = matrix.shape[0] // (matrix.shape[1] // rank)
    return jnp.where(row // n_rows == column // rank, matrix, jnp.zeros_like(matrix))


def low_of(me_ref, rows_ref, gain_ref, normed_ref, maps, width, rank):
    values = flat(rows_ref[...]).astype(jnp.float32)
    scale = lax.rsqrt(jnp.mean(values * values, axis=-1, keepdims=True) + 1e-05)
    normed_ref[...] = (values * scale * gain_ref[...].astype(jnp.float32)).astype(jnp.bfloat16)
    total = None
    for piece, down in enumerate(maps):
        part = dot(normed_ref[:, columns(me_ref, piece, len(maps), width)], flat(down), 1)
        total = part if total is None else total + part
    return own_blocks(total.astype(jnp.bfloat16), rank)


def add_update(me_ref, out_ref, rows_ref, low, maps, width):
    for piece, up in enumerate(maps):
        at = columns(me_ref, piece, len(maps), width)
        block = rows_ref[:, :, at]
        update = dot(low, flat(up)).reshape(block.shape)
        out_ref[:, :, at] = (block.astype(jnp.float32) + update).astype(jnp.bfloat16)


def layer_kernel(n, rank, width, me_ref, rows_ref, gain_ref, *refs):
    pieces, wide_refs, (out_ref, normed_ref) = refs[:n], refs[n:-2], refs[-2:]
    downs = [p[0] for p in pieces]
    low = low_of(me_ref, rows_ref, gain_ref, normed_ref, downs, width, rank)
    add_update(me_ref, out_ref, rows_ref, low, [p[1] for p in pieces], width)
    dim = rows_ref.shape[2]
    for wide_ref in wide_refs:
        for block in range(out_ref.shape[0]):
            part = pl.ds(block * LANES, LANES)
            kept = (block + 1) * LANES <= wide_ref.shape[2]
            values = wide_ref[0, :, part] if kept else jnp.zeros_like(wide_ref[0, :, :LANES])
            out_ref[block, :, dim:] = values


def block_columns(step, n_columns, width):
    row, column = rows_and_columns((n_columns, width))
    return zero_one(column == row + step * n_columns)


def low_kernel(n, rank, width, me_ref, rows_ref, gain_ref, *refs):
    pieces, out_ref, normed_ref, wide_ref = refs[:n], refs[n], refs[n + 1], refs[n + 2]
    downs = [p[...].reshape(-1, rank, width) for p in pieces]
    low = low_of(me_ref, rows_ref, gain_ref, normed_ref, downs, width, rank)
    held = rows_ref.shape[1]
    row, column = rows_and_columns((held, low.shape[0]))
    folded = dot(zero_one(column % held == row), low).astype(jnp.bfloat16)
    step = pl.program_id(0)
    mine = dot(folded, block_columns(step, folded.shape[1], wide_ref.shape[1]))

    @pl.when(step == 0)
    def _():
        wide_ref[...] = mine

    @pl.when(step > 0)
    def _():
        wide_ref[...] += mine

    @pl.when(step == pl.num_programs(0) - 1)
    def _():
        out_ref[0] = wide_ref[...].astype(out_ref.dtype)


def update_kernel(n, rank, width, first_step, me_ref, rows_ref, wide_ref, *refs):
    pieces, out_ref = refs[:n], refs[-1]
    count, held, _ = rows_ref.shape
    wide = jnp.concatenate([wide_ref[i] for i in range(wide_ref.shape[0])], axis=1)
    places = block_columns(pl.program_id(0) + first_step, count * rank, wide.shape[1])
    folded = dot(wide, places, 1).astype(jnp.bfloat16)
    row, column = rows_and_columns((count * held, held))
    low = own_blocks(dot(zero_one(row % held == column), folded).astype(jnp.bfloat16), rank)
    add_update(me_ref, out_ref, rows_ref, low, [p[...] for p in pieces], width)


def place_kernel(first, count, block_ref, *refs):
    out_ref, arrived = refs[-2], refs[-1]
    dim = out_ref.shape[2]
    copy = pltpu.make_async_copy(
        block_ref.at[:, :, pl.ds(0, dim)], out_ref.at[pl.ds(first, count)], arrived
    )
    copy.start()
    copy.wait()


def tiny_cost():
    return pl.CostEstimate(flops=1, bytes_accessed=1, transcendentals=0)


def params(mib=56):
    return pltpu.CompilerParams(vmem_limit_bytes=mib * MIB)


def per_step(first, count):
    blocks = math.gcd(first, count)
    return blocks // 2 if blocks > 4 and blocks % 2 == 0 else blocks


def blocks_of(*shape, first=0):
    zeros = (0,) * (len(shape) - 1)
    return pl.BlockSpec(shape, lambda b, s: (b + first // shape[0], *zeros))


def pair_blocks(size, rank, width, first=0):
    return pl.BlockSpec((2, size, rank, width), lambda b, s: (0, b + first // size, 0, 0))


def all_gain(dim):
    return pl.BlockSpec((1, dim), lambda b, s: (0, 0))


def layer_blocks(me, rows, first, count, gain, other, pieces, skipped, *wide):
    rank, width = pieces[0].shape[2:]
    held, dim = rows.shape[1:]
    size = per_step(first, count)
    pieces = [pieces[0], other] + pieces[1:]
    specs = [pair_blocks(size, rank, width, skipped)] * len(pieces)
    specs[1] = pair_blocks(size, rank, width, first)
    specs += [pl.BlockSpec(low.shape, lambda b, s: (0, 0, 0)) for low in wide]
    out_dim = dim + LANES * len(wide)
    return pl.pallas_call(
        functools.partial(layer_kernel, len(pieces), rank, width),
        out_shape=jax.ShapeDtypeStruct((count, held, out_dim), jnp.bfloat16),
        grid_spec=pltpu.PrefetchScalarGridSpec(
            num_scalar_prefetch=1,
            grid=(count // size,),
            in_specs=[blocks_of(size, held, dim, first=first), all_gain(dim)] + specs,
            out_specs=blocks_of(size, held, out_dim),
            scratch_shapes=[pltpu.VMEM((size * held, dim), jnp.bfloat16)],
        ),
        compiler_params=params(),
        cost_estimate=tiny_cost(),
    )(me, rows, gain, *pieces, *wide)


def low_lanes(raw, rank):
    return -(-raw * rank // LANES) * LANES


def low_blocks(me, rows, gain, other, pieces):
    count, rank, width = pieces[0].shape
    held, dim = rows.shape[1:]
    size = per_step(count, count // 2)
    lanes = low_lanes(count, rank)
    pieces = [pieces[0], other] + pieces[1:]
    specs = [blocks_of(size, rank, width)] * len(pieces)
    specs[1] = pl.BlockSpec((1, size, rank, width), lambda b, s: (0, b, 0, 0))
    return pl.pallas_call(
        functools.partial(low_kernel, len(pieces), rank, width),
        out_shape=jax.ShapeDtypeStruct((1, held, lanes), jnp.bfloat16),
        grid_spec=pltpu.PrefetchScalarGridSpec(
            num_scalar_prefetch=1,
            grid=(count // size,),
            in_specs=[blocks_of(size, held, dim), all_gain(dim)] + specs,
            out_specs=pl.BlockSpec((1, held, lanes), lambda b, s: (0, 0, 0)),
            scratch_shapes=[
                pltpu.VMEM((size * held, dim), jnp.bfloat16),
                pltpu.VMEM((held, lanes), jnp.float32),
            ],
        ),
        compiler_params=params(),
        cost_estimate=tiny_cost(),
    )(me, rows, gain, *pieces)


def update_blocks(me, rows, count, with_low, pieces, first, result):
    n, (raw, rank, width) = len(pieces), pieces[0].shape
    held, dim = rows.shape[1:]
    size = per_step(first, count) if first else per_step(count, count // 2)
    low_spec = pl.BlockSpec(
        (low_lanes(raw, rank) // LANES, held, LANES), lambda b, s: (0, 0, dim // LANES)
    )
    return pl.pallas_call(
        functools.partial(update_kernel, n, rank, width, first // size),
        out_shape=jax.ShapeDtypeStruct(result.shape, result.dtype),
        grid_spec=pltpu.PrefetchScalarGridSpec(
            num_scalar_prefetch=1,
            grid=(count // size,),
            in_specs=[blocks_of(size, held, dim), low_spec]
            + [blocks_of(size, rank, width, first=first)] * n
            + [pl.BlockSpec(memory_space=pl.ANY)],
            out_specs=blocks_of(size, held, dim, first=first),
        ),
        input_output_aliases={3 + n: 0},
        compiler_params=params(),
        cost_estimate=tiny_cost(),
    )(me, rows, with_low, *pieces, result)


def place_blocks(block, first, result, shape):
    count, held = block.shape[:2]
    into = [] if result is None else [result]
    return pl.pallas_call(
        functools.partial(place_kernel, first, count),
        out_shape=jax.ShapeDtypeStruct(shape, jnp.bfloat16),
        in_specs=[pl.BlockSpec(memory_space=pltpu.VMEM)]
        + [pl.BlockSpec(memory_space=pl.ANY)] * len(into),
        out_specs=pl.BlockSpec(memory_space=pl.ANY),
        scratch_shapes=[pltpu.SemaphoreType.DMA],
        input_output_aliases={1: 0} if into else {},
        compiler_params=params(4),
        cost_estimate=tiny_cost(),
    )(block, *into)


def norm_rows(block_rows, gain):
    values = block_rows.astype(jnp.float32)
    scale = lax.rsqrt(jnp.mean(values * values, axis=-1, keepdims=True) + 1e-05)
    return (values * scale * gain.astype(jnp.float32)).astype(jnp.bfloat16)


def apply_adapter(block_rows, gain, down_maps, up_maps):
    values = block_rows.astype(jnp.float32)
    normed = norm_rows(block_rows, gain)
    low = jnp.einsum("bnd,brd->bnr", normed, down_maps, preferred_element_type=jnp.float32).astype(
        jnp.bfloat16
    )
    update = jnp.einsum("bnr,brd->bnd", low, up_maps, preferred_element_type=jnp.float32)
    return (values + update).astype(jnp.bfloat16)


def gathered_whole(
    activations, block_expert, seq_task, norm_gain, task_embed, expert_embed, gen_down, gen_up
):
    rows = activations[0]
    expert_ids = block_expert[0, :, 0]
    n_blocks = expert_ids.shape[0]
    per_seq = n_blocks // seq_task.shape[1]
    task_ids = seq_task[0][jnp.arange(n_blocks, dtype=jnp.int32) // per_seq]
    code_all = jax.nn.silu(
        task_embed.astype(jnp.float32)[:, None, :] + expert_embed[0].astype(jnp.float32)[None]
    ).astype(jnp.bfloat16)
    code_rows = code_all[task_ids, expert_ids]
    down_part = jnp.einsum(
        "bh,hrd->brd", code_rows, gen_down[0], preferred_element_type=jnp.float32
    ).astype(jnp.bfloat16)
    up_part = jnp.einsum(
        "bh,hrd->brd", code_rows, gen_up[0], preferred_element_type=jnp.float32
    ).astype(jnp.bfloat16)
    down_full, up_full = (
        lax.all_gather(down_part, "expert", axis=2, tiled=True),
        lax.all_gather(up_part, "expert", axis=2, tiled=True),
    )
    result = apply_adapter(rows, norm_gain[0], down_full, up_full)
    return passed_along(result[None], "section", 1)


def on_device(
    activations, block_expert, seq_task, norm_gain, task_embed, expert_embed, gen_down, gen_up
):
    n_blocks, held, dim = activations.shape[1:]
    rank, width = gen_down.shape[2:]
    n_devices = lax.axis_size("expert")
    raw, early = n_blocks // 2, n_blocks // 8
    chunks = [(raw, raw + n_blocks // 4), (raw + n_blocks // 4, n_blocks)]
    aligned = held % 16 == 0 and rank % 16 == 0 and width % LANES == 0
    if not aligned or n_blocks % 32 or raw % n_devices or n_devices % CORES or n_devices // CORES != 4:
        return gathered_whole(
            activations, block_expert, seq_task, norm_gain, task_embed, expert_embed, gen_down, gen_up
        )

    rows = activations[0]
    carried = raw - early
    early_sent = passed_along(rows[carried:raw], "section", 1)
    whole, raw_down, carrier, *chunk_maps = generated(
        block_expert[0, :, 0], seq_task[0], task_embed, expert_embed, gen_down, gen_up,
        rows, raw, carried, chunks,
    )
    carrier_sent = passed_along(carrier, "section", 1)
    ups = carrier_sent[carried:].reshape(-1, held, n_devices, width).swapaxes(1, 2)
    me = jnp.reshape(lax.axis_index("expert"), (1,)).astype(jnp.int32)
    other = core_swap(whole)

    ends, swaps = [], []

    class Gather:
        def __init__(self, block):
            self.held, self.pieces = block, [block]

        def step(self, *after, before_swap=()):
            k = len(ends)
            after = [*after, *ends[max(k - 2, 0) : max(k - 1, 0)], *swaps[max(k - 3, 0) : max(k - 2, 0)]]
            ends.append(ring_step(tied(self.held, *after) if after else self.held))
            swaps.append(core_swap(tied(ends[-1], *before_swap) if before_swap else ends[-1]))
            self.held = ends[-1]
            self.pieces += [ends[-1], swaps[-1]]

    first, second = (Gather(block) for block in chunk_maps)
    downs, ups = Gather(raw_down), Gather(ups.reshape(raw, rank, width))
    first.step()
    first.step(early_sent)
    downs.step()
    first.step()
    (at, end), (middle, last) = chunks[0], (chunks[1][0] + n_blocks // 8, n_blocks)
    first_out = layer_blocks(me, rows, at, end - at, norm_gain, other, first.pieces, 0)
    first_sent = passed_along(tied(first_out, early_sent), "section", 1)
    downs.step()
    second.step()
    downs.step(first_out)
    low = low_blocks(me, rows, norm_gain, other, downs.pieces)
    second.step(before_swap=[low])
    second.step()
    second_out = layer_blocks(me, rows, end, middle - end, norm_gain, other, second.pieces, 0, low)
    second_sent = passed_along(tied(second_out, carrier_sent), "section", 1)
    third_out = layer_blocks(me, rows, middle, last - middle, norm_gain, other, second.pieces, middle - end)
    third_sent = passed_along(tied(third_out, first_sent), "section", 1)
    ups.step()
    result = place_blocks(first_sent, at, None, rows.shape)
    ups.held, result = lax.optimization_barrier((ups.held, result))
    ups.step(second_out)
    ups.step(third_out)

    maps = [ups.pieces[0], core_swap(ups.pieces[0])] + ups.pieces[1:]
    result = place_blocks(second_sent, end, result, rows.shape)
    result = update_blocks(me, early_sent, early, second_sent, maps, carried, result)
    result = update_blocks(me, carrier_sent, carried, second_sent, maps, 0, result)
    return place_blocks(third_sent, middle, result, rows.shape)[None]


def solution(mesh):
    in_specs = (
        P("section", "groups", "expert", None),
        P("section", "groups", None),
        P("section", "groups"),
        P("section", None),
        P(),
        P("section", None, None),
        P("section", None, None, "expert"),
        P("section", None, None, "expert"),
    )
    out_specs = P("section", "groups", "expert", None)
    return jax.shard_map(
        on_device, mesh=mesh, in_specs=in_specs, out_specs=out_specs, check_vma=False
    )
```

```python
import functools
import math

import jax
import jax.numpy as jnp
from jax import lax
from jax.experimental import pallas as pl
from jax.experimental.pallas import tpu as pltpu
from jax.sharding import PartitionSpec as P

CORES = 2
LANES = 128
MIB = 1024 * 1024


def passed_along(block, axis, distance):
    devices = range(lax.axis_size(axis))
    route = [((i - distance) % len(devices), i) for i in devices]
    return lax.ppermute(block, axis, route)


def chip_ring(n_chips):
    return list(range(0, n_chips, 2)) + list(range(1, n_chips, 2))[::-1]


def ring_step(block):
    order = chip_ring(lax.axis_size("expert") // CORES)
    route = []
    for at, chip in enumerate(order):
        after = order[(at + 1) % len(order)]
        route += [(chip * CORES + core, after * CORES + core) for core in range(CORES)]
    return lax.ppermute(block, "expert", route)


def core_swap(block):
    route = [(i, i ^ 1) for i in range(lax.axis_size("expert"))]
    return lax.ppermute(block, "expert", route)


def piece_owner(me, piece, n_chips):
    chip, core = me // CORES, me % CORES
    at = jnp.where(chip % 2 == 0, chip // 2, n_chips - 1 - chip // 2)
    at = (at - piece // CORES + n_chips) % n_chips
    source = jnp.where(at < (n_chips + 1) // 2, 2 * at, 2 * (n_chips - 1 - at) + 1)
    return source * CORES + (core + piece) % CORES


def tied(value, *after):
    return lax.optimization_barrier((value, *after))[0]


def rows_and_columns(shape):
    return (lax.broadcasted_iota(jnp.int32, shape, axis) for axis in (0, 1))


def zero_one(condition):
    return jnp.where(condition, 1.0, 0.0).astype(jnp.bfloat16)


def dot(a, b, contract_b=0):
    return lax.dot_general(
        a, b, (((1,), (contract_b,)), ((), ())), preferred_element_type=jnp.float32
    )


def generator_kernel(
    chunks, rank, expert_ref, task_ref, task_embed_ref, expert_embed_ref, down_ref, up_ref, rows_ref, *refs
):
    whole_ref, raw_down_ref, carrier_ref = refs[:3]
    chunk_refs = refs[3 : 3 + len(chunks)]
    code_ref, tasks_ref, experts_ref, spread_ref, down_sum, up_sum, copied = refs[3 + len(chunks) :]
    step = pl.program_id(0)
    n_blocks, per_step = code_ref.shape[0], spread_ref.shape[2]
    per_seq = n_blocks // task_ref.shape[0]
    n_rows = n_blocks * rank
    width = down_ref.shape[3]
    raw = raw_down_ref.shape[0]
    pieces = carrier_ref.shape[2] // width
    carried = carrier_ref.shape[0] - raw // pieces
    copy = pltpu.make_async_copy(
        rows_ref.at[pl.ds(0, carried)], carrier_ref.at[pl.ds(0, carried)], copied
    )

    @pl.when(step == 0)
    def _():
        copy.start()
        tasks_ref[...] = task_embed_ref[...].astype(jnp.float32)
        experts_ref[...] = expert_embed_ref[0].astype(jnp.float32)
        for block in range(n_blocks):
            task = tasks_ref[pl.ds(task_ref[block // per_seq], 1), :]
            expert = experts_ref[pl.ds(expert_ref[block], 1), :]
            code_ref[pl.ds(block, 1), :] = task + expert
        code = jax.nn.silu(code_ref[...]).astype(jnp.bfloat16)
        row, block = rows_and_columns((n_rows, n_blocks))
        repeat = zero_one(row // rank == block)
        for part in range(spread_ref.shape[0]):
            columns = code[:, part * per_step : (part + 1) * per_step]
            spread_ref[part] = dot(repeat, columns).astype(jnp.bfloat16)
        down_sum[...] = jnp.zeros_like(down_sum)
        up_sum[...] = jnp.zeros_like(up_sum)

    entry, column = rows_and_columns((per_step, per_step * rank))
    wide = dot(spread_ref[step], zero_one(column // rank == entry)).astype(jnp.bfloat16)
    row, column = rows_and_columns(wide.shape)
    wide = jnp.where(row % rank == column % rank, wide, jnp.zeros_like(wide))
    down_sum[...] += dot(wide, down_ref[0].reshape(per_step * rank, width))
    up_sum[...] += dot(wide, up_ref[0].reshape(per_step * rank, width))

    @pl.when(step == pl.num_programs(0) - 1)
    def _():
        shape = (n_blocks, rank, width)
        down = down_sum[...].astype(jnp.bfloat16).reshape(shape)
        up = up_sum[...].astype(jnp.bfloat16).reshape(shape)
        whole_ref[0], whole_ref[1] = down, up
        raw_down_ref[...] = down[:raw]
        for (first, last), ref in zip(chunks, chunk_refs):
            ref[0], ref[1] = down[first:last], up[first:last]
        for block in range(raw):
            at = pl.ds(block % pieces * width, width)
            carrier_ref[carried + block // pieces, :, at] = up[block]
        copy.wait()


def generated(expert_ids, task_ids, task_embed, expert_embed, gen_down, gen_up, rows, raw, carried, chunks):
    _, hyp, rank, width = gen_down.shape
    n_blocks, held, dim = rows.shape
    per_step = math.gcd(hyp, 64)
    n_rows = n_blocks * rank
    shapes = [(2, n_blocks, rank, width), (raw, rank, width), (carried + raw * width // dim, held, dim)]
    shapes += [(2, last - first, rank, width) for first, last in chunks]

    def whole(shape):
        return pl.BlockSpec(shape, lambda h, *_: (0,) * len(shape))

    generator = pl.BlockSpec((1, per_step, rank, width), lambda h, *_: (0, h, 0, 0))
    return pl.pallas_call(
        functools.partial(generator_kernel, chunks, rank),
        out_shape=[jax.ShapeDtypeStruct(shape, jnp.bfloat16) for shape in shapes],
        grid_spec=pltpu.PrefetchScalarGridSpec(
            num_scalar_prefetch=2,
            grid=(hyp // per_step,),
            in_specs=[
                whole(task_embed.shape),
                whole(expert_embed.shape),
                generator,
                generator,
                pl.BlockSpec(memory_space=pl.ANY),
            ],
            out_specs=[whole(shape) for shape in shapes],
            scratch_shapes=[
                pltpu.VMEM((n_blocks, hyp), jnp.float32),
                pltpu.VMEM(task_embed.shape, jnp.float32),
                pltpu.VMEM(expert_embed.shape[1:], jnp.float32),
                pltpu.VMEM((hyp // per_step, n_rows, per_step), jnp.bfloat16),
                pltpu.VMEM((n_rows, width), jnp.float32),
                pltpu.VMEM((n_rows, width), jnp.float32),
                pltpu.SemaphoreType.DMA,
            ],
        ),
        compiler_params=params(),
        cost_estimate=tiny_cost(),
    )(expert_ids, task_ids, task_embed, expert_embed, gen_down, gen_up, rows)


def columns(me_ref, piece, n_pieces, width):
    owner = piece_owner(me_ref[0], piece, n_pieces // CORES)
    return pl.ds(pl.multiple_of(owner * width, 128), width)


def flat(block):
    return block.reshape(-1, block.shape[-1])


def own_blocks(matrix, rank):
    row, column = rows_and_columns(matrix.shape)
    n_rows = matrix.shape[0] // (matrix.shape[1] // rank)
    return jnp.where(row // n_rows == column // rank, matrix, jnp.zeros_like(matrix))


def low_of(me_ref, rows_ref, gain_ref, normed_ref, maps, width, rank):
    values = flat(rows_ref[...]).astype(jnp.float32)
    scale = lax.rsqrt(jnp.mean(values * values, axis=-1, keepdims=True) + 1e-05)
    normed_ref[...] = (values * scale * gain_ref[...].astype(jnp.float32)).astype(jnp.bfloat16)
    total = None
    for piece, down in enumerate(maps):
        part = dot(normed_ref[:, columns(me_ref, piece, len(maps), width)], flat(down), 1)
        total = part if total is None else total + part
    return own_blocks(total.astype(jnp.bfloat16), rank)


def add_update(me_ref, out_ref, rows_ref, low, maps, width):
    for piece, up in enumerate(maps):
        at = columns(me_ref, piece, len(maps), width)
        block = rows_ref[:, :, at]
        update = dot(low, flat(up)).reshape(block.shape)
        out_ref[:, :, at] = (block.astype(jnp.float32) + update).astype(jnp.bfloat16)


def layer_kernel(n, rank, width, me_ref, rows_ref, gain_ref, *refs):
    downs, ups, wide_refs = refs[:n], refs[n : 2 * n], refs[2 * n : -2]
    out_ref, normed_ref = refs[-2:]
    low = low_of(me_ref, rows_ref, gain_ref, normed_ref, [p[...] for p in downs], width, rank)
    add_update(me_ref, out_ref, rows_ref, low, [p[...] for p in ups], width)
    dim = rows_ref.shape[2]
    for wide_ref in wide_refs:
        for block in range(out_ref.shape[0]):
            part = pl.ds(block * LANES, LANES)
            kept = (block + 1) * LANES <= wide_ref.shape[2]
            values = wide_ref[0, :, part] if kept else jnp.zeros_like(wide_ref[0, :, :LANES])
            out_ref[block, :, dim:] = values


def block_columns(step, n_columns, width):
    row, column = rows_and_columns((n_columns, width))
    return zero_one(column == row + step * n_columns)


def low_kernel(n, rank, width, me_ref, rows_ref, gain_ref, *refs):
    pieces, out_ref, normed_ref, wide_ref = refs[:n], refs[n], refs[n + 1], refs[n + 2]
    downs = [p[...].reshape(-1, rank, width) for p in pieces]
    low = low_of(me_ref, rows_ref, gain_ref, normed_ref, downs, width, rank)
    held = rows_ref.shape[1]
    row, column = rows_and_columns((held, low.shape[0]))
    folded = dot(zero_one(column % held == row), low).astype(jnp.bfloat16)
    step = pl.program_id(0)
    mine = dot(folded, block_columns(step, folded.shape[1], wide_ref.shape[1]))

    @pl.when(step == 0)
    def _():
        wide_ref[...] = mine

    @pl.when(step > 0)
    def _():
        wide_ref[...] += mine

    @pl.when(step == pl.num_programs(0) - 1)
    def _():
        out_ref[0] = wide_ref[...].astype(out_ref.dtype)


def update_kernel(n, rank, width, first_step, me_ref, rows_ref, wide_ref, *refs):
    pieces, out_ref = refs[:n], refs[-1]
    count, held, _ = rows_ref.shape
    wide = jnp.concatenate([wide_ref[i] for i in range(wide_ref.shape[0])], axis=1)
    places = block_columns(pl.program_id(0) + first_step, count * rank, wide.shape[1])
    folded = dot(wide, places, 1).astype(jnp.bfloat16)
    row, column = rows_and_columns((count * held, held))
    low = own_blocks(dot(zero_one(row % held == column), folded).astype(jnp.bfloat16), rank)
    add_update(me_ref, out_ref, rows_ref, low, [p[...] for p in pieces], width)


def place_kernel(first, count, block_ref, *refs):
    out_ref, arrived = refs[-2], refs[-1]
    dim = out_ref.shape[2]
    copy = pltpu.make_async_copy(
        block_ref.at[:, :, pl.ds(0, dim)], out_ref.at[pl.ds(first, count)], arrived
    )
    copy.start()
    copy.wait()


def tiny_cost():
    return pl.CostEstimate(flops=1, bytes_accessed=1, transcendentals=0)


def params(mib=56):
    return pltpu.CompilerParams(vmem_limit_bytes=mib * MIB)


def per_step(first, count):
    blocks = math.gcd(first, count)
    return blocks // 2 if blocks > 4 and blocks % 2 == 0 else blocks


def blocks_of(*shape, first=0):
    zeros = (0,) * (len(shape) - 1)
    return pl.BlockSpec(shape, lambda b, s: (b + first // shape[0], *zeros))


def half_blocks(half, size, rank, width, first=0):
    return pl.BlockSpec((None, size, rank, width), lambda b, s: (half, b + first // size, 0, 0))


def all_gain(dim):
    return pl.BlockSpec((1, dim), lambda b, s: (0, 0))


def layer_blocks(me, rows, first, count, gain, other, downs, ups, skipped, *wide):
    rank, width = downs[0].shape[-2:]
    held, dim = rows.shape[1:]
    size = per_step(first, count)
    specs, pieces = [], []
    for half, maps in enumerate((downs, ups)):
        for at, block in enumerate([maps[0], other] + maps[1:]):
            offset = first if at == 1 else skipped
            if block.ndim == 4:
                specs.append(half_blocks(half, size, rank, width, offset))
            else:
                specs.append(blocks_of(size, rank, width, first=offset))
            pieces.append(block)
    specs += [pl.BlockSpec(low.shape, lambda b, s: (0, 0, 0)) for low in wide]
    out_dim = dim + LANES * len(wide)
    return pl.pallas_call(
        functools.partial(layer_kernel, len(pieces) // 2, rank, width),
        out_shape=jax.ShapeDtypeStruct((count, held, out_dim), jnp.bfloat16),
        grid_spec=pltpu.PrefetchScalarGridSpec(
            num_scalar_prefetch=1,
            grid=(count // size,),
            in_specs=[blocks_of(size, held, dim, first=first), all_gain(dim)] + specs,
            out_specs=blocks_of(size, held, out_dim),
            scratch_shapes=[pltpu.VMEM((size * held, dim), jnp.bfloat16)],
        ),
        compiler_params=params(),
        cost_estimate=tiny_cost(),
    )(me, rows, gain, *pieces, *wide)


def low_lanes(raw, rank):
    return -(-raw * rank // LANES) * LANES


def low_blocks(me, rows, gain, other, pieces):
    count, rank, width = pieces[0].shape
    held, dim = rows.shape[1:]
    size = per_step(count, count // 2)
    lanes = low_lanes(count, rank)
    pieces = [pieces[0], other] + pieces[1:]
    specs = [blocks_of(size, rank, width)] * len(pieces)
    specs[1] = pl.BlockSpec((1, size, rank, width), lambda b, s: (0, b, 0, 0))
    return pl.pallas_call(
        functools.partial(low_kernel, len(pieces), rank, width),
        out_shape=jax.ShapeDtypeStruct((1, held, lanes), jnp.bfloat16),
        grid_spec=pltpu.PrefetchScalarGridSpec(
            num_scalar_prefetch=1,
            grid=(count // size,),
            in_specs=[blocks_of(size, held, dim), all_gain(dim)] + specs,
            out_specs=pl.BlockSpec((1, held, lanes), lambda b, s: (0, 0, 0)),
            scratch_shapes=[
                pltpu.VMEM((size * held, dim), jnp.bfloat16),
                pltpu.VMEM((held, lanes), jnp.float32),
            ],
        ),
        compiler_params=params(),
        cost_estimate=tiny_cost(),
    )(me, rows, gain, *pieces)


def update_blocks(me, rows, count, with_low, pieces, first, result):
    n, (raw, rank, width) = len(pieces), pieces[0].shape
    held, dim = rows.shape[1:]
    size = per_step(first, count) if first else per_step(count, count // 2)
    low_spec = pl.BlockSpec(
        (low_lanes(raw, rank) // LANES, held, LANES), lambda b, s: (0, 0, dim // LANES)
    )
    return pl.pallas_call(
        functools.partial(update_kernel, n, rank, width, first // size),
        out_shape=jax.ShapeDtypeStruct(result.shape, result.dtype),
        grid_spec=pltpu.PrefetchScalarGridSpec(
            num_scalar_prefetch=1,
            grid=(count // size,),
            in_specs=[blocks_of(size, held, dim), low_spec]
            + [blocks_of(size, rank, width, first=first)] * n
            + [pl.BlockSpec(memory_space=pl.ANY)],
            out_specs=blocks_of(size, held, dim, first=first),
        ),
        input_output_aliases={3 + n: 0},
        compiler_params=params(),
        cost_estimate=tiny_cost(),
    )(me, rows, with_low, *pieces, result)


def place_blocks(block, first, result, shape):
    count, held = block.shape[:2]
    into = [] if result is None else [result]
    return pl.pallas_call(
        functools.partial(place_kernel, first, count),
        out_shape=jax.ShapeDtypeStruct(shape, jnp.bfloat16),
        in_specs=[pl.BlockSpec(memory_space=pltpu.VMEM)]
        + [pl.BlockSpec(memory_space=pl.ANY)] * len(into),
        out_specs=pl.BlockSpec(memory_space=pl.ANY),
        scratch_shapes=[pltpu.SemaphoreType.DMA],
        input_output_aliases={1: 0} if into else {},
        compiler_params=params(4),
        cost_estimate=tiny_cost(),
    )(block, *into)


def norm_rows(block_rows, gain):
    values = block_rows.astype(jnp.float32)
    scale = lax.rsqrt(jnp.mean(values * values, axis=-1, keepdims=True) + 1e-05)
    return (values * scale * gain.astype(jnp.float32)).astype(jnp.bfloat16)


def apply_adapter(block_rows, gain, down_maps, up_maps):
    values = block_rows.astype(jnp.float32)
    normed = norm_rows(block_rows, gain)
    low = jnp.einsum("bnd,brd->bnr", normed, down_maps, preferred_element_type=jnp.float32).astype(
        jnp.bfloat16
    )
    update = jnp.einsum("bnr,brd->bnd", low, up_maps, preferred_element_type=jnp.float32)
    return (values + update).astype(jnp.bfloat16)


def gathered_whole(
    activations, block_expert, seq_task, norm_gain, task_embed, expert_embed, gen_down, gen_up
):
    rows = activations[0]
    expert_ids = block_expert[0, :, 0]
    n_blocks = expert_ids.shape[0]
    per_seq = n_blocks // seq_task.shape[1]
    task_ids = seq_task[0][jnp.arange(n_blocks, dtype=jnp.int32) // per_seq]
    code_all = jax.nn.silu(
        task_embed.astype(jnp.float32)[:, None, :] + expert_embed[0].astype(jnp.float32)[None]
    ).astype(jnp.bfloat16)
    code_rows = code_all[task_ids, expert_ids]
    down_part = jnp.einsum(
        "bh,hrd->brd", code_rows, gen_down[0], preferred_element_type=jnp.float32
    ).astype(jnp.bfloat16)
    up_part = jnp.einsum(
        "bh,hrd->brd", code_rows, gen_up[0], preferred_element_type=jnp.float32
    ).astype(jnp.bfloat16)
    down_full, up_full = (
        lax.all_gather(down_part, "expert", axis=2, tiled=True),
        lax.all_gather(up_part, "expert", axis=2, tiled=True),
    )
    result = apply_adapter(rows, norm_gain[0], down_full, up_full)
    return passed_along(result[None], "section", 1)


def on_device(
    activations, block_expert, seq_task, norm_gain, task_embed, expert_embed, gen_down, gen_up
):
    n_blocks, held, dim = activations.shape[1:]
    rank, width = gen_down.shape[2:]
    n_devices = lax.axis_size("expert")
    raw, early = n_blocks // 2, n_blocks // 8
    chunks = [(raw, raw + n_blocks // 4), (raw + n_blocks // 4, n_blocks)]
    aligned = held % 16 == 0 and rank % 16 == 0 and width % LANES == 0
    if not aligned or n_blocks % 32 or raw % n_devices or n_devices % CORES or n_devices // CORES != 4:
        return gathered_whole(
            activations, block_expert, seq_task, norm_gain, task_embed, expert_embed, gen_down, gen_up
        )

    rows = activations[0]
    carried = raw - early
    early_sent = passed_along(rows[carried:raw], "section", 1)
    whole, raw_down, carrier, *chunk_maps = generated(
        block_expert[0, :, 0], seq_task[0], task_embed, expert_embed, gen_down, gen_up,
        rows, raw, carried, chunks,
    )
    carrier_sent = passed_along(carrier, "section", 1)
    ups = carrier_sent[carried:].reshape(-1, held, n_devices, width).swapaxes(1, 2)
    me = jnp.reshape(lax.axis_index("expert"), (1,)).astype(jnp.int32)
    other = core_swap(whole)

    ends, swaps = [], []

    class Gather:
        def __init__(self, block):
            self.held, self.pieces = block, [block]

        def step(self, *after, before_swap=(), split=False):
            k = len(ends)
            after = [*after, *ends[max(k - 2, 0) : max(k - 1, 0)], *swaps[max(k - 3, 0) : max(k - 2, 0)]]
            ends.append(ring_step(tied(self.held, *after) if after else self.held))
            if split:
                self.pieces += [ends[-1], [core_swap(half) for half in ends[-1]]]
                swaps.append(self.pieces[-1][0])
                return
            swaps.append(core_swap(tied(ends[-1], *before_swap) if before_swap else ends[-1]))
            self.held = ends[-1]
            self.pieces += [ends[-1], swaps[-1]]

    first, second = (Gather(block) for block in chunk_maps)
    downs, ups = Gather(raw_down), Gather(ups.reshape(raw, rank, width))
    (at, end), (middle, last) = chunks[0], (chunks[1][0] + n_blocks // 8, n_blocks)
    result = None
    first.step()
    first.step(early_sent)
    downs.step()
    first.step()
    first_out = layer_blocks(me, rows, at, end - at, norm_gain, other, first.pieces, first.pieces, 0)
    first_sent = passed_along(tied(first_out, early_sent), "section", 1)
    second.step()
    downs.step()
    downs.step(first_out)
    low = low_blocks(me, rows, norm_gain, other, downs.pieces)
    second.step(before_swap=[low])
    second.step(split=True)
    maps = second.pieces[:-1] + second.pieces[-1][:1], second.pieces[:-1] + second.pieces[-1][1:]
    second_out = layer_blocks(me, rows, end, middle - end, norm_gain, other, *maps, 0, low)
    second_sent = passed_along(tied(second_out, carrier_sent), "section", 1)
    third_out = layer_blocks(me, rows, middle, last - middle, norm_gain, other, *maps, middle - end)
    third_sent = passed_along(tied(third_out, first_sent), "section", 1)
    ups.step()
    ups.step(second_out)
    result = place_blocks(first_sent, at, None, rows.shape)
    ups.held, result = lax.optimization_barrier((ups.held, result))
    ups.step(third_out)

    maps = [ups.pieces[0], core_swap(ups.pieces[0])] + ups.pieces[1:]
    result = place_blocks(second_sent, end, result, rows.shape)
    result = update_blocks(me, early_sent, early, second_sent, maps, carried, result)
    result = update_blocks(me, carrier_sent, carried, second_sent, maps, 0, result)
    return place_blocks(third_sent, middle, result, rows.shape)[None]


def solution(mesh):
    in_specs = (
        P("section", "groups", "expert", None),
        P("section", "groups", None),
        P("section", "groups"),
        P("section", None),
        P(),
        P("section", None, None),
        P("section", None, None, "expert"),
        P("section", None, None, "expert"),
    )
    out_specs = P("section", "groups", "expert", None)
    return jax.shard_map(
        on_device, mesh=mesh, in_specs=in_specs, out_specs=out_specs, check_vma=False
    )
```

```python
import functools
import math

import jax
import jax.numpy as jnp
from jax import lax
from jax.experimental import pallas as pl
from jax.experimental.pallas import tpu as pltpu
from jax.sharding import PartitionSpec as P

CORES = 2
LANES = 128
MIB = 1024 * 1024


def passed_along(block, axis, distance):
    devices = range(lax.axis_size(axis))
    route = [((i - distance) % len(devices), i) for i in devices]
    return lax.ppermute(block, axis, route)


def chip_ring(n_chips):
    return list(range(0, n_chips, 2)) + list(range(1, n_chips, 2))[::-1]


def ring_step(block):
    order = chip_ring(lax.axis_size("expert") // CORES)
    route = []
    for at, chip in enumerate(order):
        after = order[(at + 1) % len(order)]
        route += [(chip * CORES + core, after * CORES + core) for core in range(CORES)]
    return lax.ppermute(block, "expert", route)


def core_swap(block):
    route = [(i, i ^ 1) for i in range(lax.axis_size("expert"))]
    return lax.ppermute(block, "expert", route)


def piece_owner(me, piece, n_chips):
    chip, core = me // CORES, me % CORES
    at = jnp.where(chip % 2 == 0, chip // 2, n_chips - 1 - chip // 2)
    at = (at - piece // CORES + n_chips) % n_chips
    source = jnp.where(at < (n_chips + 1) // 2, 2 * at, 2 * (n_chips - 1 - at) + 1)
    return source * CORES + (core + piece) % CORES


def tied(value, *after):
    return lax.optimization_barrier((value, *after))[0]


def rows_and_columns(shape):
    return (lax.broadcasted_iota(jnp.int32, shape, axis) for axis in (0, 1))


def zero_one(condition):
    return jnp.where(condition, 1.0, 0.0).astype(jnp.bfloat16)


def dot(a, b, contract_b=0):
    return lax.dot_general(
        a, b, (((1,), (contract_b,)), ((), ())), preferred_element_type=jnp.float32
    )


def generator_kernel(
    chunks, rank, expert_ref, task_ref, task_embed_ref, expert_embed_ref, down_ref, up_ref, rows_ref, *refs
):
    whole_ref, raw_down_ref, carrier_ref = refs[:3]
    chunk_refs = refs[3 : 3 + len(chunks)]
    code_ref, tasks_ref, experts_ref, spread_ref, down_sum, up_sum, copied = refs[3 + len(chunks) :]
    step = pl.program_id(0)
    n_blocks, per_step = code_ref.shape[0], spread_ref.shape[2]
    per_seq = n_blocks // task_ref.shape[0]
    n_rows = n_blocks * rank
    width = down_ref.shape[3]
    raw = raw_down_ref.shape[0]
    pieces = carrier_ref.shape[2] // width
    carried = carrier_ref.shape[0] - raw // pieces
    copy = pltpu.make_async_copy(
        rows_ref.at[pl.ds(0, carried)], carrier_ref.at[pl.ds(0, carried)], copied
    )

    @pl.when(step == 0)
    def _():
        copy.start()
        tasks_ref[...] = task_embed_ref[...].astype(jnp.float32)
        experts_ref[...] = expert_embed_ref[0].astype(jnp.float32)
        for block in range(n_blocks):
            task = tasks_ref[pl.ds(task_ref[block // per_seq], 1), :]
            expert = experts_ref[pl.ds(expert_ref[block], 1), :]
            code_ref[pl.ds(block, 1), :] = task + expert
        code = jax.nn.silu(code_ref[...]).astype(jnp.bfloat16)
        row, block = rows_and_columns((n_rows, n_blocks))
        repeat = zero_one(row // rank == block)
        for part in range(spread_ref.shape[0]):
            columns = code[:, part * per_step : (part + 1) * per_step]
            spread_ref[part] = dot(repeat, columns).astype(jnp.bfloat16)
        down_sum[...] = jnp.zeros_like(down_sum)
        up_sum[...] = jnp.zeros_like(up_sum)

    entry, column = rows_and_columns((per_step, per_step * rank))
    wide = dot(spread_ref[step], zero_one(column // rank == entry)).astype(jnp.bfloat16)
    row, column = rows_and_columns(wide.shape)
    wide = jnp.where(row % rank == column % rank, wide, jnp.zeros_like(wide))
    down_sum[...] += dot(wide, down_ref[0].reshape(per_step * rank, width))
    up_sum[...] += dot(wide, up_ref[0].reshape(per_step * rank, width))

    @pl.when(step == pl.num_programs(0) - 1)
    def _():
        shape = (n_blocks, rank, width)
        down = down_sum[...].astype(jnp.bfloat16).reshape(shape)
        up = up_sum[...].astype(jnp.bfloat16).reshape(shape)
        whole_ref[0], whole_ref[1] = down, up
        raw_down_ref[...] = down[:raw]
        for (first, last), ref in zip(chunks, chunk_refs):
            ref[0], ref[1] = down[first:last], up[first:last]
        for block in range(raw):
            at = pl.ds(block % pieces * width, width)
            carrier_ref[carried + block // pieces, :, at] = up[block]
        copy.wait()


def generated(expert_ids, task_ids, task_embed, expert_embed, gen_down, gen_up, rows, raw, carried, chunks):
    _, hyp, rank, width = gen_down.shape
    n_blocks, held, dim = rows.shape
    per_step = math.gcd(hyp, 64)
    n_rows = n_blocks * rank
    shapes = [(2, n_blocks, rank, width), (raw, rank, width), (carried + raw * width // dim, held, dim)]
    shapes += [(2, last - first, rank, width) for first, last in chunks]

    def whole(shape):
        return pl.BlockSpec(shape, lambda h, *_: (0,) * len(shape))

    generator = pl.BlockSpec((1, per_step, rank, width), lambda h, *_: (0, h, 0, 0))
    return pl.pallas_call(
        functools.partial(generator_kernel, chunks, rank),
        out_shape=[jax.ShapeDtypeStruct(shape, jnp.bfloat16) for shape in shapes],
        grid_spec=pltpu.PrefetchScalarGridSpec(
            num_scalar_prefetch=2,
            grid=(hyp // per_step,),
            in_specs=[
                whole(task_embed.shape),
                whole(expert_embed.shape),
                generator,
                generator,
                pl.BlockSpec(memory_space=pl.ANY),
            ],
            out_specs=[whole(shape) for shape in shapes],
            scratch_shapes=[
                pltpu.VMEM((n_blocks, hyp), jnp.float32),
                pltpu.VMEM(task_embed.shape, jnp.float32),
                pltpu.VMEM(expert_embed.shape[1:], jnp.float32),
                pltpu.VMEM((hyp // per_step, n_rows, per_step), jnp.bfloat16),
                pltpu.VMEM((n_rows, width), jnp.float32),
                pltpu.VMEM((n_rows, width), jnp.float32),
                pltpu.SemaphoreType.DMA,
            ],
        ),
        compiler_params=params(),
        cost_estimate=tiny_cost(),
    )(expert_ids, task_ids, task_embed, expert_embed, gen_down, gen_up, rows)


def columns(me_ref, piece, n_pieces, width):
    owner = piece_owner(me_ref[0], piece, n_pieces // CORES)
    return pl.ds(pl.multiple_of(owner * width, 128), width)


def flat(block):
    return block.reshape(-1, block.shape[-1])


def own_blocks(matrix, rank):
    row, column = rows_and_columns(matrix.shape)
    n_rows = matrix.shape[0] // (matrix.shape[1] // rank)
    return jnp.where(row // n_rows == column // rank, matrix, jnp.zeros_like(matrix))


def low_of(me_ref, rows_ref, gain_ref, normed_ref, maps, width, rank):
    values = flat(rows_ref[...]).astype(jnp.float32)
    scale = lax.rsqrt(jnp.mean(values * values, axis=-1, keepdims=True) + 1e-05)
    normed_ref[...] = (values * scale * gain_ref[...].astype(jnp.float32)).astype(jnp.bfloat16)
    total = None
    for piece, down in enumerate(maps):
        part = dot(normed_ref[:, columns(me_ref, piece, len(maps), width)], flat(down), 1)
        total = part if total is None else total + part
    return own_blocks(total.astype(jnp.bfloat16), rank)


def add_update(me_ref, out_ref, rows_ref, low, maps, width):
    for piece, up in enumerate(maps):
        at = columns(me_ref, piece, len(maps), width)
        block = rows_ref[:, :, at]
        update = dot(low, flat(up)).reshape(block.shape)
        out_ref[:, :, at] = (block.astype(jnp.float32) + update).astype(jnp.bfloat16)


def layer_kernel(n, rank, width, me_ref, rows_ref, gain_ref, *refs):
    downs, ups, wide_refs = refs[:n], refs[n : 2 * n], refs[2 * n : -2]
    out_ref, normed_ref = refs[-2:]
    low = low_of(me_ref, rows_ref, gain_ref, normed_ref, [p[...] for p in downs], width, rank)
    add_update(me_ref, out_ref, rows_ref, low, [p[...] for p in ups], width)
    dim = rows_ref.shape[2]
    for wide_ref in wide_refs:
        for block in range(out_ref.shape[0]):
            part = pl.ds(block * LANES, LANES)
            kept = (block + 1) * LANES <= wide_ref.shape[2]
            values = wide_ref[0, :, part] if kept else jnp.zeros_like(wide_ref[0, :, :LANES])
            out_ref[block, :, dim:] = values


def block_columns(step, n_columns, width):
    row, column = rows_and_columns((n_columns, width))
    return zero_one(column == row + step * n_columns)


def low_kernel(n, rank, width, me_ref, rows_ref, gain_ref, *refs):
    pieces, out_ref, normed_ref, wide_ref = refs[:n], refs[n], refs[n + 1], refs[n + 2]
    downs = [p[...].reshape(-1, rank, width) for p in pieces]
    low = low_of(me_ref, rows_ref, gain_ref, normed_ref, downs, width, rank)
    held = rows_ref.shape[1]
    row, column = rows_and_columns((held, low.shape[0]))
    folded = dot(zero_one(column % held == row), low).astype(jnp.bfloat16)
    step = pl.program_id(0)
    mine = dot(folded, block_columns(step, folded.shape[1], wide_ref.shape[1]))

    @pl.when(step == 0)
    def _():
        wide_ref[...] = mine

    @pl.when(step > 0)
    def _():
        wide_ref[...] += mine

    @pl.when(step == pl.num_programs(0) - 1)
    def _():
        out_ref[0] = wide_ref[...].astype(out_ref.dtype)


def update_kernel(n, rank, me_ref, carrier_ref, early_ref, wide_ref, *refs):
    pieces, out_ref = refs[:n], refs[-1]
    count, held, _ = early_ref.shape
    step, last = pl.program_id(0), pl.num_programs(0) - 1
    width = pieces[0].shape[2]
    wide = jnp.concatenate([wide_ref[i] for i in range(wide_ref.shape[0])], axis=1)
    places = block_columns(step, count * rank, wide.shape[1])
    folded = dot(wide, places, 1).astype(jnp.bfloat16)
    row, column = rows_and_columns((count * held, held))
    low = own_blocks(dot(zero_one(row % held == column), folded).astype(jnp.bfloat16), rank)
    maps = [p[...] for p in pieces]

    @pl.when(step < last)
    def _():
        add_update(me_ref, out_ref, carrier_ref, low, maps, width)

    @pl.when(step == last)
    def _():
        add_update(me_ref, out_ref, early_ref, low, maps, width)


def place_kernel(first, count, block_ref, *refs):
    out_ref, arrived = refs[-2], refs[-1]
    dim = out_ref.shape[2]
    copy = pltpu.make_async_copy(
        block_ref.at[:, :, pl.ds(0, dim)], out_ref.at[pl.ds(first, count)], arrived
    )
    copy.start()
    copy.wait()


def tiny_cost():
    return pl.CostEstimate(flops=1, bytes_accessed=1, transcendentals=0)


def params(mib=56):
    return pltpu.CompilerParams(vmem_limit_bytes=mib * MIB)


def per_step(first, count):
    blocks = math.gcd(first, count)
    return blocks // 2 if blocks > 4 and blocks % 2 == 0 else blocks


def blocks_of(*shape, first=0):
    zeros = (0,) * (len(shape) - 1)
    return pl.BlockSpec(shape, lambda b, s: (b + first // shape[0], *zeros))


def half_blocks(half, size, rank, width, first=0):
    return pl.BlockSpec((None, size, rank, width), lambda b, s: (half, b + first // size, 0, 0))


def all_gain(dim):
    return pl.BlockSpec((1, dim), lambda b, s: (0, 0))


def layer_blocks(me, rows, first, count, gain, other, downs, ups, skipped, *wide):
    rank, width = downs[0].shape[-2:]
    held, dim = rows.shape[1:]
    size = per_step(first, count)
    specs, pieces = [], []
    for half, maps in enumerate((downs, ups)):
        for at, block in enumerate([maps[0], other] + maps[1:]):
            offset = first if at == 1 else skipped
            if block.ndim == 4:
                specs.append(half_blocks(half, size, rank, width, offset))
            else:
                specs.append(blocks_of(size, rank, width, first=offset))
            pieces.append(block)
    specs += [pl.BlockSpec(low.shape, lambda b, s: (0, 0, 0)) for low in wide]
    out_dim = dim + LANES * len(wide)
    return pl.pallas_call(
        functools.partial(layer_kernel, len(pieces) // 2, rank, width),
        out_shape=jax.ShapeDtypeStruct((count, held, out_dim), jnp.bfloat16),
        grid_spec=pltpu.PrefetchScalarGridSpec(
            num_scalar_prefetch=1,
            grid=(count // size,),
            in_specs=[blocks_of(size, held, dim, first=first), all_gain(dim)] + specs,
            out_specs=blocks_of(size, held, out_dim),
            scratch_shapes=[pltpu.VMEM((size * held, dim), jnp.bfloat16)],
        ),
        compiler_params=params(),
        cost_estimate=tiny_cost(),
    )(me, rows, gain, *pieces, *wide)


def low_lanes(raw, rank):
    return -(-raw * rank // LANES) * LANES


def low_blocks(me, rows, gain, other, pieces):
    count, rank, width = pieces[0].shape
    held, dim = rows.shape[1:]
    size = per_step(count, count // 2)
    lanes = low_lanes(count, rank)
    pieces = [pieces[0], other] + pieces[1:]
    specs = [blocks_of(size, rank, width)] * len(pieces)
    specs[1] = pl.BlockSpec((1, size, rank, width), lambda b, s: (0, b, 0, 0))
    return pl.pallas_call(
        functools.partial(low_kernel, len(pieces), rank, width),
        out_shape=jax.ShapeDtypeStruct((1, held, lanes), jnp.bfloat16),
        grid_spec=pltpu.PrefetchScalarGridSpec(
            num_scalar_prefetch=1,
            grid=(count // size,),
            in_specs=[blocks_of(size, held, dim), all_gain(dim)] + specs,
            out_specs=pl.BlockSpec((1, held, lanes), lambda b, s: (0, 0, 0)),
            scratch_shapes=[
                pltpu.VMEM((size * held, dim), jnp.bfloat16),
                pltpu.VMEM((held, lanes), jnp.float32),
            ],
        ),
        compiler_params=params(),
        cost_estimate=tiny_cost(),
    )(me, rows, gain, *pieces)


def update_blocks(me, carrier, early, with_low, pieces, result):
    n, (raw, rank, width) = len(pieces), pieces[0].shape
    size, held, dim = early.shape
    steps = raw // size
    low_spec = pl.BlockSpec(
        (low_lanes(raw, rank) // LANES, held, LANES), lambda b, s: (0, 0, dim // LANES)
    )
    return pl.pallas_call(
        functools.partial(update_kernel, n, rank),
        out_shape=jax.ShapeDtypeStruct(result.shape, result.dtype),
        grid_spec=pltpu.PrefetchScalarGridSpec(
            num_scalar_prefetch=1,
            grid=(steps,),
            in_specs=[
                pl.BlockSpec((size, held, dim), lambda b, s: (jnp.minimum(b, steps - 2), 0, 0)),
                pl.BlockSpec((size, held, dim), lambda b, s: (0, 0, 0)),
                low_spec,
            ]
            + [blocks_of(size, rank, width)] * n
            + [pl.BlockSpec(memory_space=pl.ANY)],
            out_specs=blocks_of(size, held, dim),
        ),
        input_output_aliases={4 + n: 0},
        compiler_params=params(),
        cost_estimate=tiny_cost(),
    )(me, carrier, early, with_low, *pieces, result)


def place_blocks(block, first, result, shape):
    count, held = block.shape[:2]
    into = [] if result is None else [result]
    return pl.pallas_call(
        functools.partial(place_kernel, first, count),
        out_shape=jax.ShapeDtypeStruct(shape, jnp.bfloat16),
        in_specs=[pl.BlockSpec(memory_space=pltpu.VMEM)]
        + [pl.BlockSpec(memory_space=pl.ANY)] * len(into),
        out_specs=pl.BlockSpec(memory_space=pl.ANY),
        scratch_shapes=[pltpu.SemaphoreType.DMA],
        input_output_aliases={1: 0} if into else {},
        compiler_params=params(4),
        cost_estimate=tiny_cost(),
    )(block, *into)


def norm_rows(block_rows, gain):
    values = block_rows.astype(jnp.float32)
    scale = lax.rsqrt(jnp.mean(values * values, axis=-1, keepdims=True) + 1e-05)
    return (values * scale * gain.astype(jnp.float32)).astype(jnp.bfloat16)


def apply_adapter(block_rows, gain, down_maps, up_maps):
    values = block_rows.astype(jnp.float32)
    normed = norm_rows(block_rows, gain)
    low = jnp.einsum("bnd,brd->bnr", normed, down_maps, preferred_element_type=jnp.float32).astype(
        jnp.bfloat16
    )
    update = jnp.einsum("bnr,brd->bnd", low, up_maps, preferred_element_type=jnp.float32)
    return (values + update).astype(jnp.bfloat16)


def gathered_whole(
    activations, block_expert, seq_task, norm_gain, task_embed, expert_embed, gen_down, gen_up
):
    rows = activations[0]
    expert_ids = block_expert[0, :, 0]
    n_blocks = expert_ids.shape[0]
    per_seq = n_blocks // seq_task.shape[1]
    task_ids = seq_task[0][jnp.arange(n_blocks, dtype=jnp.int32) // per_seq]
    code_all = jax.nn.silu(
        task_embed.astype(jnp.float32)[:, None, :] + expert_embed[0].astype(jnp.float32)[None]
    ).astype(jnp.bfloat16)
    code_rows = code_all[task_ids, expert_ids]
    down_part = jnp.einsum(
        "bh,hrd->brd", code_rows, gen_down[0], preferred_element_type=jnp.float32
    ).astype(jnp.bfloat16)
    up_part = jnp.einsum(
        "bh,hrd->brd", code_rows, gen_up[0], preferred_element_type=jnp.float32
    ).astype(jnp.bfloat16)
    down_full, up_full = (
        lax.all_gather(down_part, "expert", axis=2, tiled=True),
        lax.all_gather(up_part, "expert", axis=2, tiled=True),
    )
    result = apply_adapter(rows, norm_gain[0], down_full, up_full)
    return passed_along(result[None], "section", 1)


def on_device(
    activations, block_expert, seq_task, norm_gain, task_embed, expert_embed, gen_down, gen_up
):
    n_blocks, held, dim = activations.shape[1:]
    rank, width = gen_down.shape[2:]
    n_devices = lax.axis_size("expert")
    raw, early = n_blocks // 2, n_blocks // 8
    chunks = [(raw, raw + n_blocks // 4), (raw + n_blocks // 4, n_blocks)]
    aligned = held % 16 == 0 and rank % 16 == 0 and width % LANES == 0
    if not aligned or n_blocks % 32 or raw % n_devices or n_devices % CORES or n_devices // CORES != 4:
        return gathered_whole(
            activations, block_expert, seq_task, norm_gain, task_embed, expert_embed, gen_down, gen_up
        )

    rows = activations[0]
    carried = raw - early
    early_sent = passed_along(rows[carried:raw], "section", 1)
    whole, raw_down, carrier, *chunk_maps = generated(
        block_expert[0, :, 0], seq_task[0], task_embed, expert_embed, gen_down, gen_up,
        rows, raw, carried, chunks,
    )
    carrier_sent = passed_along(carrier, "section", 1)
    ups = carrier_sent[carried:].reshape(-1, held, n_devices, width).swapaxes(1, 2)
    me = jnp.reshape(lax.axis_index("expert"), (1,)).astype(jnp.int32)
    other = core_swap(whole)

    ends, swaps = [], []

    class Gather:
        def __init__(self, block):
            self.held, self.pieces = block, [block]

        def step(self, *after, before_swap=(), split=False):
            k = len(ends)
            after = [*after, *ends[max(k - 2, 0) : max(k - 1, 0)], *swaps[max(k - 3, 0) : max(k - 2, 0)]]
            ends.append(ring_step(tied(self.held, *after) if after else self.held))
            if split:
                self.pieces += [ends[-1], [core_swap(half) for half in ends[-1]]]
                swaps.append(self.pieces[-1][0])
                return
            swaps.append(core_swap(tied(ends[-1], *before_swap) if before_swap else ends[-1]))
            self.held = ends[-1]
            self.pieces += [ends[-1], swaps[-1]]

    first, second = (Gather(block) for block in chunk_maps)
    downs, ups = Gather(raw_down), Gather(ups.reshape(raw, rank, width))
    (at, end), (middle, last) = chunks[0], (chunks[1][0] + n_blocks // 8, n_blocks)
    result = None
    first.step()
    first.step(early_sent)
    downs.step()
    first.step()
    first_out = layer_blocks(me, rows, at, end - at, norm_gain, other, first.pieces, first.pieces, 0)
    first_sent = passed_along(tied(first_out, early_sent), "section", 1)
    second.step()
    downs.step()
    downs.step(first_out)
    low = low_blocks(me, rows, norm_gain, other, downs.pieces)
    second.step(before_swap=[low])
    second.step(split=True)
    maps = second.pieces[:-1] + second.pieces[-1][:1], second.pieces[:-1] + second.pieces[-1][1:]
    second_out = layer_blocks(me, rows, end, middle - end, norm_gain, other, *maps, 0, low)
    second_sent = passed_along(tied(second_out, carrier_sent), "section", 1)
    third_out = layer_blocks(me, rows, middle, last - middle, norm_gain, other, *maps, middle - end)
    third_sent = passed_along(tied(third_out, first_sent), "section", 1)
    ups.step()
    ups.step(second_out)
    result = place_blocks(first_sent, at, None, rows.shape)
    ups.held, result = lax.optimization_barrier((ups.held, result))
    ups.step(third_out)

    maps = [ups.pieces[0], core_swap(ups.pieces[0])] + ups.pieces[1:]
    result = place_blocks(second_sent, end, result, rows.shape)
    result = update_blocks(me, carrier_sent, early_sent, second_sent, maps, result)
    return place_blocks(third_sent, middle, result, rows.shape)[None]


def solution(mesh):
    in_specs = (
        P("section", "groups", "expert", None),
        P("section", "groups", None),
        P("section", "groups"),
        P("section", None),
        P(),
        P("section", None, None),
        P("section", None, None, "expert"),
        P("section", None, None, "expert"),
    )
    out_specs = P("section", "groups", "expert", None)
    return jax.shard_map(
        on_device, mesh=mesh, in_specs=in_specs, out_specs=out_specs, check_vma=False
    )
```

```python
import functools
import math

import jax
import jax.numpy as jnp
from jax import lax
from jax.experimental import pallas as pl
from jax.experimental.pallas import tpu as pltpu
from jax.sharding import PartitionSpec as P

CORES = 2
LANES = 128
MIB = 1024 * 1024


def passed_along(block, axis, distance):
    devices = range(lax.axis_size(axis))
    route = [((i - distance) % len(devices), i) for i in devices]
    return lax.ppermute(block, axis, route)


def chip_ring(n_chips):
    return list(range(0, n_chips, 2)) + list(range(1, n_chips, 2))[::-1]


def ring_step(block):
    order = chip_ring(lax.axis_size("expert") // CORES)
    route = []
    for at, chip in enumerate(order):
        after = order[(at + 1) % len(order)]
        route += [(chip * CORES + core, after * CORES + core) for core in range(CORES)]
    return lax.ppermute(block, "expert", route)


def core_swap(block):
    route = [(i, i ^ 1) for i in range(lax.axis_size("expert"))]
    return lax.ppermute(block, "expert", route)


def piece_owner(me, piece, n_chips):
    chip, core = me // CORES, me % CORES
    at = jnp.where(chip % 2 == 0, chip // 2, n_chips - 1 - chip // 2)
    at = (at - piece // CORES + n_chips) % n_chips
    source = jnp.where(at < (n_chips + 1) // 2, 2 * at, 2 * (n_chips - 1 - at) + 1)
    return source * CORES + (core + piece) % CORES


def tied(value, *after):
    return lax.optimization_barrier((value, *after))[0]


def rows_and_columns(shape):
    return (lax.broadcasted_iota(jnp.int32, shape, axis) for axis in (0, 1))


def zero_one(condition):
    return jnp.where(condition, 1.0, 0.0).astype(jnp.bfloat16)


def dot(a, b, contract_b=0):
    return lax.dot_general(
        a, b, (((1,), (contract_b,)), ((), ())), preferred_element_type=jnp.float32
    )


def generator_kernel(
    chunks, rank, expert_ref, task_ref, task_embed_ref, expert_embed_ref, down_ref, up_ref, rows_ref, *refs
):
    whole_ref, raw_down_ref, carrier_ref = refs[:3]
    chunk_refs = refs[3 : 3 + len(chunks)]
    code_ref, tasks_ref, experts_ref, spread_ref, down_sum, up_sum, copied = refs[3 + len(chunks) :]
    step = pl.program_id(0)
    n_blocks, per_step = code_ref.shape[0], spread_ref.shape[2]
    per_seq = n_blocks // task_ref.shape[0]
    n_rows = n_blocks * rank
    width = down_ref.shape[3]
    raw = raw_down_ref.shape[0]
    pieces = carrier_ref.shape[2] // width
    carried = carrier_ref.shape[0] - raw // pieces
    copy = pltpu.make_async_copy(
        rows_ref.at[pl.ds(0, carried)], carrier_ref.at[pl.ds(0, carried)], copied
    )

    @pl.when(step == 0)
    def _():
        copy.start()
        tasks_ref[...] = task_embed_ref[...].astype(jnp.float32)
        experts_ref[...] = expert_embed_ref[0].astype(jnp.float32)
        for block in range(n_blocks):
            task = tasks_ref[pl.ds(task_ref[block // per_seq], 1), :]
            expert = experts_ref[pl.ds(expert_ref[block], 1), :]
            code_ref[pl.ds(block, 1), :] = task + expert
        code = jax.nn.silu(code_ref[...]).astype(jnp.bfloat16)
        row, block = rows_and_columns((n_rows, n_blocks))
        repeat = zero_one(row // rank == block)
        for part in range(spread_ref.shape[0]):
            columns = code[:, part * per_step : (part + 1) * per_step]
            spread_ref[part] = dot(repeat, columns).astype(jnp.bfloat16)
        down_sum[...] = jnp.zeros_like(down_sum)
        up_sum[...] = jnp.zeros_like(up_sum)

    entry, column = rows_and_columns((per_step, per_step * rank))
    wide = dot(spread_ref[step], zero_one(column // rank == entry)).astype(jnp.bfloat16)
    row, column = rows_and_columns(wide.shape)
    wide = jnp.where(row % rank == column % rank, wide, jnp.zeros_like(wide))
    down_sum[...] += dot(wide, down_ref[0].reshape(per_step * rank, width))
    up_sum[...] += dot(wide, up_ref[0].reshape(per_step * rank, width))

    @pl.when(step == pl.num_programs(0) - 1)
    def _():
        shape = (n_blocks, rank, width)
        down = down_sum[...].astype(jnp.bfloat16).reshape(shape)
        up = up_sum[...].astype(jnp.bfloat16).reshape(shape)
        whole_ref[0], whole_ref[1] = down, up
        raw_down_ref[...] = down[:raw]
        for (first, last), ref in zip(chunks, chunk_refs):
            ref[0], ref[1] = down[first:last], up[first:last]
        for block in range(raw):
            at = pl.ds(block % pieces * width, width)
            carrier_ref[carried + block // pieces, :, at] = up[block]
        copy.wait()


def generated(expert_ids, task_ids, task_embed, expert_embed, gen_down, gen_up, rows, raw, carried, chunks):
    _, hyp, rank, width = gen_down.shape
    n_blocks, held, dim = rows.shape
    per_step = math.gcd(hyp, 64)
    n_rows = n_blocks * rank
    shapes = [(2, n_blocks, rank, width), (raw, rank, width), (carried + raw * width // dim, held, dim)]
    shapes += [(2, last - first, rank, width) for first, last in chunks]

    def whole(shape):
        return pl.BlockSpec(shape, lambda h, *_: (0,) * len(shape))

    generator = pl.BlockSpec((1, per_step, rank, width), lambda h, *_: (0, h, 0, 0))
    return pl.pallas_call(
        functools.partial(generator_kernel, chunks, rank),
        out_shape=[jax.ShapeDtypeStruct(shape, jnp.bfloat16) for shape in shapes],
        grid_spec=pltpu.PrefetchScalarGridSpec(
            num_scalar_prefetch=2,
            grid=(hyp // per_step,),
            in_specs=[
                whole(task_embed.shape),
                whole(expert_embed.shape),
                generator,
                generator,
                pl.BlockSpec(memory_space=pl.ANY),
            ],
            out_specs=[whole(shape) for shape in shapes],
            scratch_shapes=[
                pltpu.VMEM((n_blocks, hyp), jnp.float32),
                pltpu.VMEM(task_embed.shape, jnp.float32),
                pltpu.VMEM(expert_embed.shape[1:], jnp.float32),
                pltpu.VMEM((hyp // per_step, n_rows, per_step), jnp.bfloat16),
                pltpu.VMEM((n_rows, width), jnp.float32),
                pltpu.VMEM((n_rows, width), jnp.float32),
                pltpu.SemaphoreType.DMA,
            ],
        ),
        compiler_params=params(),
        cost_estimate=tiny_cost(),
    )(expert_ids, task_ids, task_embed, expert_embed, gen_down, gen_up, rows)


def columns(me_ref, piece, n_pieces, width):
    owner = piece_owner(me_ref[0], piece, n_pieces // CORES)
    return pl.ds(pl.multiple_of(owner * width, 128), width)


def flat(block):
    return block.reshape(-1, block.shape[-1])


def own_blocks(matrix, rank):
    row, column = rows_and_columns(matrix.shape)
    n_rows = matrix.shape[0] // (matrix.shape[1] // rank)
    return jnp.where(row // n_rows == column // rank, matrix, jnp.zeros_like(matrix))


def low_of(me_ref, rows_ref, gain_ref, normed_ref, maps, width, rank):
    values = flat(rows_ref[...]).astype(jnp.float32)
    scale = lax.rsqrt(jnp.mean(values * values, axis=-1, keepdims=True) + 1e-05)
    normed_ref[...] = (values * scale * gain_ref[...].astype(jnp.float32)).astype(jnp.bfloat16)
    total = None
    for piece, down in enumerate(maps):
        part = dot(normed_ref[:, columns(me_ref, piece, len(maps), width)], flat(down), 1)
        total = part if total is None else total + part
    return own_blocks(total.astype(jnp.bfloat16), rank)


def add_update(me_ref, out_ref, rows_ref, low, maps, width):
    for piece, up in enumerate(maps):
        at = columns(me_ref, piece, len(maps), width)
        block = rows_ref[:, :, at]
        update = dot(low, flat(up)).reshape(block.shape)
        out_ref[:, :, at] = (block.astype(jnp.float32) + update).astype(jnp.bfloat16)


def layer_kernel(n, rank, width, me_ref, rows_ref, gain_ref, *refs):
    downs, ups, wide_refs = refs[:n], refs[n : 2 * n], refs[2 * n : -2]
    out_ref, normed_ref = refs[-2:]
    low = low_of(me_ref, rows_ref, gain_ref, normed_ref, [p[...] for p in downs], width, rank)
    add_update(me_ref, out_ref, rows_ref, low, [p[...] for p in ups], width)
    dim = rows_ref.shape[2]
    for wide_ref in wide_refs:
        for block in range(out_ref.shape[0]):
            part = pl.ds(block * LANES, LANES)
            kept = (block + 1) * LANES <= wide_ref.shape[2]
            values = wide_ref[0, :, part] if kept else jnp.zeros_like(wide_ref[0, :, :LANES])
            out_ref[block, :, dim:] = values


def block_columns(step, n_columns, width):
    row, column = rows_and_columns((n_columns, width))
    return zero_one(column == row + step * n_columns)


def low_kernel(n, rank, width, me_ref, rows_ref, gain_ref, *refs):
    pieces, out_ref, normed_ref, wide_ref = refs[:n], refs[n], refs[n + 1], refs[n + 2]
    downs = [p[...].reshape(-1, rank, width) for p in pieces]
    low = low_of(me_ref, rows_ref, gain_ref, normed_ref, downs, width, rank)
    held = rows_ref.shape[1]
    row, column = rows_and_columns((held, low.shape[0]))
    folded = dot(zero_one(column % held == row), low).astype(jnp.bfloat16)
    step = pl.program_id(0)
    mine = dot(folded, block_columns(step, folded.shape[1], wide_ref.shape[1]))

    @pl.when(step == 0)
    def _():
        wide_ref[...] = mine

    @pl.when(step > 0)
    def _():
        wide_ref[...] += mine

    @pl.when(step == pl.num_programs(0) - 1)
    def _():
        out_ref[0] = wide_ref[...].astype(out_ref.dtype)


def update_kernel(n, rank, me_ref, carrier_ref, early_ref, wide_ref, *refs):
    pieces, out_ref = refs[:n], refs[-1]
    count, held, _ = early_ref.shape
    step, last = pl.program_id(0), pl.num_programs(0) - 1
    width = pieces[0].shape[2]
    wide = jnp.concatenate([wide_ref[i] for i in range(wide_ref.shape[0])], axis=1)
    places = block_columns(step, count * rank, wide.shape[1])
    folded = dot(wide, places, 1).astype(jnp.bfloat16)
    row, column = rows_and_columns((count * held, held))
    low = own_blocks(dot(zero_one(row % held == column), folded).astype(jnp.bfloat16), rank)
    maps = [p[...] for p in pieces]

    @pl.when(step < last)
    def _():
        add_update(me_ref, out_ref, carrier_ref, low, maps, width)

    @pl.when(step == last)
    def _():
        add_update(me_ref, out_ref, early_ref, low, maps, width)


def place_kernel(first, count, block_ref, *refs):
    out_ref, arrived = refs[-2], refs[-1]
    dim = out_ref.shape[2]
    copy = pltpu.make_async_copy(
        block_ref.at[:, :, pl.ds(0, dim)], out_ref.at[pl.ds(first, count)], arrived
    )
    copy.start()
    copy.wait()


def tiny_cost():
    return pl.CostEstimate(flops=1, bytes_accessed=1, transcendentals=0)


def params(mib=56):
    return pltpu.CompilerParams(vmem_limit_bytes=mib * MIB)


def per_step(first, count):
    blocks = math.gcd(first, count)
    return blocks // 2 if blocks > 4 and blocks % 2 == 0 else blocks


def blocks_of(*shape, first=0):
    zeros = (0,) * (len(shape) - 1)
    return pl.BlockSpec(shape, lambda b, s: (b + first // shape[0], *zeros))


def half_blocks(half, size, rank, width, first=0):
    return pl.BlockSpec((None, size, rank, width), lambda b, s: (half, b + first // size, 0, 0))


def all_gain(dim):
    return pl.BlockSpec((1, dim), lambda b, s: (0, 0))


def layer_blocks(me, rows, first, count, gain, other, downs, ups, skipped, *wide):
    rank, width = downs[0].shape[-2:]
    held, dim = rows.shape[1:]
    size = per_step(first, count)
    specs, pieces = [], []
    for half, maps in enumerate((downs, ups)):
        for at, block in enumerate([maps[0], other] + maps[1:]):
            offset = first if at == 1 else skipped
            if block.ndim == 4:
                specs.append(half_blocks(half, size, rank, width, offset))
            else:
                specs.append(blocks_of(size, rank, width, first=offset))
            pieces.append(block)
    specs += [pl.BlockSpec(low.shape, lambda b, s: (0, 0, 0)) for low in wide]
    out_dim = dim + LANES * len(wide)
    return pl.pallas_call(
        functools.partial(layer_kernel, len(pieces) // 2, rank, width),
        out_shape=jax.ShapeDtypeStruct((count, held, out_dim), jnp.bfloat16),
        grid_spec=pltpu.PrefetchScalarGridSpec(
            num_scalar_prefetch=1,
            grid=(count // size,),
            in_specs=[blocks_of(size, held, dim, first=first), all_gain(dim)] + specs,
            out_specs=blocks_of(size, held, out_dim),
            scratch_shapes=[pltpu.VMEM((size * held, dim), jnp.bfloat16)],
        ),
        compiler_params=params(),
        cost_estimate=tiny_cost(),
    )(me, rows, gain, *pieces, *wide)


def low_lanes(raw, rank):
    return -(-raw * rank // LANES) * LANES


def low_blocks(me, rows, gain, other, pieces):
    count, rank, width = pieces[0].shape
    held, dim = rows.shape[1:]
    size = per_step(count, count // 2)
    lanes = low_lanes(count, rank)
    pieces = [pieces[0], other] + pieces[1:]
    specs = [blocks_of(size, rank, width)] * len(pieces)
    specs[1] = pl.BlockSpec((1, size, rank, width), lambda b, s: (0, b, 0, 0))
    return pl.pallas_call(
        functools.partial(low_kernel, len(pieces), rank, width),
        out_shape=jax.ShapeDtypeStruct((1, held, lanes), jnp.bfloat16),
        grid_spec=pltpu.PrefetchScalarGridSpec(
            num_scalar_prefetch=1,
            grid=(count // size,),
            in_specs=[blocks_of(size, held, dim), all_gain(dim)] + specs,
            out_specs=pl.BlockSpec((1, held, lanes), lambda b, s: (0, 0, 0)),
            scratch_shapes=[
                pltpu.VMEM((size * held, dim), jnp.bfloat16),
                pltpu.VMEM((held, lanes), jnp.float32),
            ],
        ),
        compiler_params=params(),
        cost_estimate=tiny_cost(),
    )(me, rows, gain, *pieces)


def update_blocks(me, carrier, early, with_low, pieces, result):
    n, (raw, rank, width) = len(pieces), pieces[0].shape
    size, held, dim = early.shape
    steps = raw // size
    low_spec = pl.BlockSpec(
        (low_lanes(raw, rank) // LANES, held, LANES), lambda b, s: (0, 0, dim // LANES)
    )
    return pl.pallas_call(
        functools.partial(update_kernel, n, rank),
        out_shape=jax.ShapeDtypeStruct(result.shape, result.dtype),
        grid_spec=pltpu.PrefetchScalarGridSpec(
            num_scalar_prefetch=1,
            grid=(steps,),
            in_specs=[
                pl.BlockSpec((size, held, dim), lambda b, s: (jnp.minimum(b, steps - 2), 0, 0)),
                pl.BlockSpec((size, held, dim), lambda b, s: (0, 0, 0)),
                low_spec,
            ]
            + [blocks_of(size, rank, width)] * n
            + [pl.BlockSpec(memory_space=pl.ANY)],
            out_specs=blocks_of(size, held, dim),
        ),
        input_output_aliases={4 + n: 0},
        compiler_params=params(),
        cost_estimate=tiny_cost(),
    )(me, carrier, early, with_low, *pieces, result)


def place_blocks(block, first, result, shape):
    count, held = block.shape[:2]
    into = [] if result is None else [result]
    return pl.pallas_call(
        functools.partial(place_kernel, first, count),
        out_shape=jax.ShapeDtypeStruct(shape, jnp.bfloat16),
        in_specs=[pl.BlockSpec(memory_space=pltpu.VMEM)]
        + [pl.BlockSpec(memory_space=pl.ANY)] * len(into),
        out_specs=pl.BlockSpec(memory_space=pl.ANY),
        scratch_shapes=[pltpu.SemaphoreType.DMA],
        input_output_aliases={1: 0} if into else {},
        compiler_params=params(4),
        cost_estimate=tiny_cost(),
    )(block, *into)


def norm_rows(block_rows, gain):
    values = block_rows.astype(jnp.float32)
    scale = lax.rsqrt(jnp.mean(values * values, axis=-1, keepdims=True) + 1e-05)
    return (values * scale * gain.astype(jnp.float32)).astype(jnp.bfloat16)


def apply_adapter(block_rows, gain, down_maps, up_maps):
    values = block_rows.astype(jnp.float32)
    normed = norm_rows(block_rows, gain)
    low = jnp.einsum("bnd,brd->bnr", normed, down_maps, preferred_element_type=jnp.float32).astype(
        jnp.bfloat16
    )
    update = jnp.einsum("bnr,brd->bnd", low, up_maps, preferred_element_type=jnp.float32)
    return (values + update).astype(jnp.bfloat16)


def gathered_whole(
    activations, block_expert, seq_task, norm_gain, task_embed, expert_embed, gen_down, gen_up
):
    rows = activations[0]
    expert_ids = block_expert[0, :, 0]
    n_blocks = expert_ids.shape[0]
    per_seq = n_blocks // seq_task.shape[1]
    task_ids = seq_task[0][jnp.arange(n_blocks, dtype=jnp.int32) // per_seq]
    code_all = jax.nn.silu(
        task_embed.astype(jnp.float32)[:, None, :] + expert_embed[0].astype(jnp.float32)[None]
    ).astype(jnp.bfloat16)
    code_rows = code_all[task_ids, expert_ids]
    down_part = jnp.einsum(
        "bh,hrd->brd", code_rows, gen_down[0], preferred_element_type=jnp.float32
    ).astype(jnp.bfloat16)
    up_part = jnp.einsum(
        "bh,hrd->brd", code_rows, gen_up[0], preferred_element_type=jnp.float32
    ).astype(jnp.bfloat16)
    down_full, up_full = (
        lax.all_gather(down_part, "expert", axis=2, tiled=True),
        lax.all_gather(up_part, "expert", axis=2, tiled=True),
    )
    result = apply_adapter(rows, norm_gain[0], down_full, up_full)
    return passed_along(result[None], "section", 1)


def on_device(
    activations, block_expert, seq_task, norm_gain, task_embed, expert_embed, gen_down, gen_up
):
    n_blocks, held, dim = activations.shape[1:]
    rank, width = gen_down.shape[2:]
    n_devices = lax.axis_size("expert")
    raw, early = n_blocks // 2, n_blocks // 8
    chunks = [(raw, raw + n_blocks // 4), (raw + n_blocks // 4, n_blocks)]
    aligned = held % 16 == 0 and rank % 16 == 0 and width % LANES == 0
    if not aligned or n_blocks % 32 or raw % n_devices or n_devices % CORES or n_devices // CORES != 4:
        return gathered_whole(
            activations, block_expert, seq_task, norm_gain, task_embed, expert_embed, gen_down, gen_up
        )

    rows = activations[0]
    carried = raw - early
    early_sent = passed_along(rows[carried:raw], "section", 1)
    whole, raw_down, carrier, *chunk_maps = generated(
        block_expert[0, :, 0], seq_task[0], task_embed, expert_embed, gen_down, gen_up,
        rows, raw, carried, chunks,
    )
    carrier_sent = passed_along(carrier, "section", 1)
    ups = carrier_sent[carried:].reshape(-1, held, n_devices, width).swapaxes(1, 2)
    me = jnp.reshape(lax.axis_index("expert"), (1,)).astype(jnp.int32)
    other = core_swap(whole)

    ends, swaps = [], []

    class Gather:
        def __init__(self, block):
            self.held, self.pieces = block, [block]

        def step(self, *after, before_swap=(), split=False):
            k = len(ends)
            after = [*after, *ends[max(k - 2, 0) : max(k - 1, 0)], *swaps[max(k - 3, 0) : max(k - 2, 0)]]
            ends.append(ring_step(tied(self.held, *after) if after else self.held))
            if split:
                self.pieces += [ends[-1], [core_swap(half) for half in ends[-1]]]
                swaps.append(self.pieces[-1][0])
                return
            swaps.append(core_swap(tied(ends[-1], *before_swap) if before_swap else ends[-1]))
            self.held = ends[-1]
            self.pieces += [ends[-1], swaps[-1]]

    first, second = (Gather(block) for block in chunk_maps)
    downs, ups = Gather(raw_down), Gather(ups.reshape(raw, rank, width))
    (at, end), (middle, last) = chunks[0], (chunks[1][0] + n_blocks // 8, n_blocks)
    result = None
    first.step()
    first.step(early_sent)
    downs.step()
    first.step()
    first_out = layer_blocks(me, rows, at, end - at, norm_gain, other, first.pieces, first.pieces, 0)
    first_sent = passed_along(tied(first_out, early_sent), "section", 1)
    second.step()
    downs.step()
    downs.step(first_out)
    low = low_blocks(me, rows, norm_gain, other, downs.pieces)
    second.step(before_swap=[low])
    second.step(split=True)
    maps = second.pieces[:-1] + second.pieces[-1][:1], second.pieces[:-1] + second.pieces[-1][1:]
    second_out = layer_blocks(me, rows, end, middle - end, norm_gain, other, *maps, 0, low)
    second_sent = passed_along(tied(second_out, carrier_sent), "section", 1)
    third_out = layer_blocks(me, rows, middle, last - middle, norm_gain, other, *maps, middle - end)
    third_sent = passed_along(tied(third_out, first_sent), "section", 1)
    ups.step()
    ups.step()
    result = place_blocks(first_sent, at, None, rows.shape)
    ups.held, result = lax.optimization_barrier((ups.held, result))
    ups.step(second_out, third_out)

    maps = [ups.pieces[0], core_swap(ups.pieces[0])] + ups.pieces[1:]
    result = place_blocks(second_sent, end, result, rows.shape)
    result = update_blocks(me, carrier_sent, early_sent, second_sent, maps, result)
    return place_blocks(third_sent, middle, result, rows.shape)[None]


def solution(mesh):
    in_specs = (
        P("section", "groups", "expert", None),
        P("section", "groups", None),
        P("section", "groups"),
        P("section", None),
        P(),
        P("section", None, None),
        P("section", None, None, "expert"),
        P("section", None, None, "expert"),
    )
    out_specs = P("section", "groups", "expert", None)
    return jax.shard_map(
        on_device, mesh=mesh, in_specs=in_specs, out_specs=out_specs, check_vma=False
    )
```

```python
import functools
import math

import jax
import jax.numpy as jnp
from jax import lax
from jax.experimental import pallas as pl
from jax.experimental.pallas import tpu as pltpu
from jax.sharding import PartitionSpec as P

CORES = 2
LANES = 128
MIB = 1024 * 1024


def passed_along(block, axis, distance):
    devices = range(lax.axis_size(axis))
    route = [((i - distance) % len(devices), i) for i in devices]
    return lax.ppermute(block, axis, route)


def chip_ring(n_chips):
    return list(range(0, n_chips, 2)) + list(range(1, n_chips, 2))[::-1]


def ring_step(block):
    order = chip_ring(lax.axis_size("expert") // CORES)
    route = []
    for at, chip in enumerate(order):
        after = order[(at + 1) % len(order)]
        route += [(chip * CORES + core, after * CORES + core) for core in range(CORES)]
    return lax.ppermute(block, "expert", route)


def core_swap(block):
    route = [(i, i ^ 1) for i in range(lax.axis_size("expert"))]
    return lax.ppermute(block, "expert", route)


def piece_owner(me, piece, n_chips):
    chip, core = me // CORES, me % CORES
    at = jnp.where(chip % 2 == 0, chip // 2, n_chips - 1 - chip // 2)
    at = (at - piece // CORES + n_chips) % n_chips
    source = jnp.where(at < (n_chips + 1) // 2, 2 * at, 2 * (n_chips - 1 - at) + 1)
    return source * CORES + (core + piece) % CORES


def tied(value, *after):
    return lax.optimization_barrier((value, *after))[0]


def rows_and_columns(shape):
    return (lax.broadcasted_iota(jnp.int32, shape, axis) for axis in (0, 1))


def zero_one(condition):
    return jnp.where(condition, 1.0, 0.0).astype(jnp.bfloat16)


def dot(a, b, contract_b=0):
    return lax.dot_general(
        a, b, (((1,), (contract_b,)), ((), ())), preferred_element_type=jnp.float32
    )


def generator_kernel(
    chunks, rank, expert_ref, task_ref, task_embed_ref, expert_embed_ref, down_ref, up_ref, rows_ref, *refs
):
    whole_ref, raw_down_ref, carrier_ref = refs[:3]
    chunk_refs = refs[3 : 3 + len(chunks)]
    code_ref, tasks_ref, experts_ref, spread_ref, down_sum, up_sum, copied = refs[3 + len(chunks) :]
    step = pl.program_id(0)
    n_blocks, per_step = code_ref.shape[0], spread_ref.shape[2]
    per_seq = n_blocks // task_ref.shape[0]
    n_rows = n_blocks * rank
    width = down_ref.shape[3]
    raw = raw_down_ref.shape[0]
    pieces = carrier_ref.shape[2] // width
    carried = carrier_ref.shape[0] - raw // pieces
    copy = pltpu.make_async_copy(
        rows_ref.at[pl.ds(0, carried)], carrier_ref.at[pl.ds(0, carried)], copied
    )

    @pl.when(step == 0)
    def _():
        copy.start()
        tasks_ref[...] = task_embed_ref[...].astype(jnp.float32)
        experts_ref[...] = expert_embed_ref[0].astype(jnp.float32)
        for block in range(n_blocks):
            task = tasks_ref[pl.ds(task_ref[block // per_seq], 1), :]
            expert = experts_ref[pl.ds(expert_ref[block], 1), :]
            code_ref[pl.ds(block, 1), :] = task + expert
        code = jax.nn.silu(code_ref[...]).astype(jnp.bfloat16)
        row, block = rows_and_columns((n_rows, n_blocks))
        repeat = zero_one(row // rank == block)
        for part in range(spread_ref.shape[0]):
            columns = code[:, part * per_step : (part + 1) * per_step]
            spread_ref[part] = dot(repeat, columns).astype(jnp.bfloat16)
        down_sum[...] = jnp.zeros_like(down_sum)
        up_sum[...] = jnp.zeros_like(up_sum)

    entry, column = rows_and_columns((per_step, per_step * rank))
    wide = dot(spread_ref[step], zero_one(column // rank == entry)).astype(jnp.bfloat16)
    row, column = rows_and_columns(wide.shape)
    wide = jnp.where(row % rank == column % rank, wide, jnp.zeros_like(wide))
    down_sum[...] += dot(wide, down_ref[0].reshape(per_step * rank, width))
    up_sum[...] += dot(wide, up_ref[0].reshape(per_step * rank, width))

    @pl.when(step == pl.num_programs(0) - 1)
    def _():
        shape = (n_blocks, rank, width)
        down = down_sum[...].astype(jnp.bfloat16).reshape(shape)
        up = up_sum[...].astype(jnp.bfloat16).reshape(shape)
        whole_ref[0], whole_ref[1] = down, up
        raw_down_ref[...] = down[:raw]
        for (first, last), ref in zip(chunks, chunk_refs):
            ref[0], ref[1] = down[first:last], up[first:last]
        for block in range(raw):
            at = pl.ds(block % pieces * width, width)
            carrier_ref[carried + block // pieces, :, at] = up[block]
        copy.wait()


def generated(expert_ids, task_ids, task_embed, expert_embed, gen_down, gen_up, rows, raw, carried, chunks):
    _, hyp, rank, width = gen_down.shape
    n_blocks, held, dim = rows.shape
    per_step = math.gcd(hyp, 64)
    n_rows = n_blocks * rank
    shapes = [(2, n_blocks, rank, width), (raw, rank, width), (carried + raw * width // dim, held, dim)]
    shapes += [(2, last - first, rank, width) for first, last in chunks]

    def whole(shape):
        return pl.BlockSpec(shape, lambda h, *_: (0,) * len(shape))

    generator = pl.BlockSpec((1, per_step, rank, width), lambda h, *_: (0, h, 0, 0))
    return pl.pallas_call(
        functools.partial(generator_kernel, chunks, rank),
        out_shape=[jax.ShapeDtypeStruct(shape, jnp.bfloat16) for shape in shapes],
        grid_spec=pltpu.PrefetchScalarGridSpec(
            num_scalar_prefetch=2,
            grid=(hyp // per_step,),
            in_specs=[
                whole(task_embed.shape),
                whole(expert_embed.shape),
                generator,
                generator,
                pl.BlockSpec(memory_space=pl.ANY),
            ],
            out_specs=[whole(shape) for shape in shapes],
            scratch_shapes=[
                pltpu.VMEM((n_blocks, hyp), jnp.float32),
                pltpu.VMEM(task_embed.shape, jnp.float32),
                pltpu.VMEM(expert_embed.shape[1:], jnp.float32),
                pltpu.VMEM((hyp // per_step, n_rows, per_step), jnp.bfloat16),
                pltpu.VMEM((n_rows, width), jnp.float32),
                pltpu.VMEM((n_rows, width), jnp.float32),
                pltpu.SemaphoreType.DMA,
            ],
        ),
        compiler_params=params(),
        cost_estimate=tiny_cost(),
    )(expert_ids, task_ids, task_embed, expert_embed, gen_down, gen_up, rows)


def columns(me_ref, piece, n_pieces, width):
    owner = piece_owner(me_ref[0], piece, n_pieces // CORES)
    return pl.ds(pl.multiple_of(owner * width, 128), width)


def flat(block):
    return block.reshape(-1, block.shape[-1])


def own_blocks(matrix, rank):
    row, column = rows_and_columns(matrix.shape)
    n_rows = matrix.shape[0] // (matrix.shape[1] // rank)
    return jnp.where(row // n_rows == column // rank, matrix, jnp.zeros_like(matrix))


def low_of(me_ref, rows_ref, gain_ref, normed_ref, maps, width, rank):
    values = flat(rows_ref[...]).astype(jnp.float32)
    scale = lax.rsqrt(jnp.mean(values * values, axis=-1, keepdims=True) + 1e-05)
    normed_ref[...] = (values * scale * gain_ref[...].astype(jnp.float32)).astype(jnp.bfloat16)
    total = None
    for piece, down in enumerate(maps):
        part = dot(normed_ref[:, columns(me_ref, piece, len(maps), width)], flat(down), 1)
        total = part if total is None else total + part
    return own_blocks(total.astype(jnp.bfloat16), rank)


def add_update(me_ref, out_ref, rows_ref, low, maps, width):
    for piece, up in enumerate(maps):
        at = columns(me_ref, piece, len(maps), width)
        block = rows_ref[:, :, at]
        update = dot(low, flat(up)).reshape(block.shape)
        out_ref[:, :, at] = (block.astype(jnp.float32) + update).astype(jnp.bfloat16)


def layer_kernel(n, rank, width, me_ref, rows_ref, gain_ref, *refs):
    downs, ups, wide_refs = refs[:n], refs[n : 2 * n], refs[2 * n : -2]
    out_ref, normed_ref = refs[-2:]
    low = low_of(me_ref, rows_ref, gain_ref, normed_ref, [p[...] for p in downs], width, rank)
    add_update(me_ref, out_ref, rows_ref, low, [p[...] for p in ups], width)
    dim = rows_ref.shape[2]
    for wide_ref in wide_refs:
        for block in range(out_ref.shape[0]):
            part = pl.ds(block * LANES, LANES)
            kept = (block + 1) * LANES <= wide_ref.shape[2]
            values = wide_ref[0, :, part] if kept else jnp.zeros_like(wide_ref[0, :, :LANES])
            out_ref[block, :, dim:] = values


def block_columns(step, n_columns, width):
    row, column = rows_and_columns((n_columns, width))
    return zero_one(column == row + step * n_columns)


def low_kernel(n, rank, width, me_ref, rows_ref, gain_ref, *refs):
    pieces, out_ref, normed_ref, wide_ref = refs[:n], refs[n], refs[n + 1], refs[n + 2]
    downs = [p[...].reshape(-1, rank, width) for p in pieces]
    low = low_of(me_ref, rows_ref, gain_ref, normed_ref, downs, width, rank)
    held = rows_ref.shape[1]
    row, column = rows_and_columns((held, low.shape[0]))
    folded = dot(zero_one(column % held == row), low).astype(jnp.bfloat16)
    step = pl.program_id(0)
    mine = dot(folded, block_columns(step, folded.shape[1], wide_ref.shape[1]))

    @pl.when(step == 0)
    def _():
        wide_ref[...] = mine

    @pl.when(step > 0)
    def _():
        wide_ref[...] += mine

    @pl.when(step == pl.num_programs(0) - 1)
    def _():
        out_ref[0] = wide_ref[...].astype(out_ref.dtype)


def update_kernel(n, rank, me_ref, carrier_ref, early_ref, wide_ref, *refs):
    pieces, out_ref = refs[:n], refs[-1]
    count, held, _ = early_ref.shape
    step, last = pl.program_id(0), pl.num_programs(0) - 1
    width = pieces[0].shape[2]
    wide = jnp.concatenate([wide_ref[i] for i in range(wide_ref.shape[0])], axis=1)
    places = block_columns(step, count * rank, wide.shape[1])
    folded = dot(wide, places, 1).astype(jnp.bfloat16)
    row, column = rows_and_columns((count * held, held))
    low = own_blocks(dot(zero_one(row % held == column), folded).astype(jnp.bfloat16), rank)
    maps = [p[...] for p in pieces]

    @pl.when(step < last)
    def _():
        add_update(me_ref, out_ref, carrier_ref, low, maps, width)

    @pl.when(step == last)
    def _():
        add_update(me_ref, out_ref, early_ref, low, maps, width)


def place_kernel(first, count, block_ref, *refs):
    out_ref, arrived = refs[-2], refs[-1]
    dim = out_ref.shape[2]
    copy = pltpu.make_async_copy(
        block_ref.at[:, :, pl.ds(0, dim)], out_ref.at[pl.ds(first, count)], arrived
    )
    copy.start()
    copy.wait()


def tiny_cost():
    return pl.CostEstimate(flops=1, bytes_accessed=1, transcendentals=0)


def params(mib=56):
    return pltpu.CompilerParams(vmem_limit_bytes=mib * MIB)


def per_step(first, count):
    blocks = math.gcd(first, count)
    return blocks // 2 if blocks > 4 and blocks % 2 == 0 else blocks


def blocks_of(*shape, first=0):
    zeros = (0,) * (len(shape) - 1)
    return pl.BlockSpec(shape, lambda b, s: (b + first // shape[0], *zeros))


def half_blocks(half, size, rank, width, first=0):
    return pl.BlockSpec((None, size, rank, width), lambda b, s: (half, b + first // size, 0, 0))


def all_gain(dim):
    return pl.BlockSpec((1, dim), lambda b, s: (0, 0))


def layer_blocks(me, rows, first, count, gain, other, downs, ups, skipped, *wide):
    rank, width = downs[0].shape[-2:]
    held, dim = rows.shape[1:]
    size = per_step(first, count)
    specs, pieces = [], []
    for half, maps in enumerate((downs, ups)):
        for at, block in enumerate([maps[0], other] + maps[1:]):
            offset = first if at == 1 else skipped
            if block.ndim == 4:
                specs.append(half_blocks(half, size, rank, width, offset))
            else:
                specs.append(blocks_of(size, rank, width, first=offset))
            pieces.append(block)
    specs += [pl.BlockSpec(low.shape, lambda b, s: (0, 0, 0)) for low in wide]
    out_dim = dim + LANES * len(wide)
    return pl.pallas_call(
        functools.partial(layer_kernel, len(pieces) // 2, rank, width),
        out_shape=jax.ShapeDtypeStruct((count, held, out_dim), jnp.bfloat16),
        grid_spec=pltpu.PrefetchScalarGridSpec(
            num_scalar_prefetch=1,
            grid=(count // size,),
            in_specs=[blocks_of(size, held, dim, first=first), all_gain(dim)] + specs,
            out_specs=blocks_of(size, held, out_dim),
            scratch_shapes=[pltpu.VMEM((size * held, dim), jnp.bfloat16)],
        ),
        compiler_params=params(),
        cost_estimate=tiny_cost(),
    )(me, rows, gain, *pieces, *wide)


def low_lanes(raw, rank):
    return -(-raw * rank // LANES) * LANES


def low_blocks(me, rows, gain, other, pieces):
    count, rank, width = pieces[0].shape
    held, dim = rows.shape[1:]
    size = per_step(count, count // 2)
    lanes = low_lanes(count, rank)
    pieces = [pieces[0], other] + pieces[1:]
    specs = [blocks_of(size, rank, width)] * len(pieces)
    specs[1] = pl.BlockSpec((1, size, rank, width), lambda b, s: (0, b, 0, 0))
    return pl.pallas_call(
        functools.partial(low_kernel, len(pieces), rank, width),
        out_shape=jax.ShapeDtypeStruct((1, held, lanes), jnp.bfloat16),
        grid_spec=pltpu.PrefetchScalarGridSpec(
            num_scalar_prefetch=1,
            grid=(count // size,),
            in_specs=[blocks_of(size, held, dim), all_gain(dim)] + specs,
            out_specs=pl.BlockSpec((1, held, lanes), lambda b, s: (0, 0, 0)),
            scratch_shapes=[
                pltpu.VMEM((size * held, dim), jnp.bfloat16),
                pltpu.VMEM((held, lanes), jnp.float32),
            ],
        ),
        compiler_params=params(),
        cost_estimate=tiny_cost(),
    )(me, rows, gain, *pieces)


def update_blocks(me, carrier, early, with_low, pieces, result):
    n, (raw, rank, width) = len(pieces), pieces[0].shape
    size, held, dim = early.shape
    steps = raw // size
    low_spec = pl.BlockSpec(
        (low_lanes(raw, rank) // LANES, held, LANES), lambda b, s: (0, 0, dim // LANES)
    )
    return pl.pallas_call(
        functools.partial(update_kernel, n, rank),
        out_shape=jax.ShapeDtypeStruct(result.shape, result.dtype),
        grid_spec=pltpu.PrefetchScalarGridSpec(
            num_scalar_prefetch=1,
            grid=(steps,),
            in_specs=[
                pl.BlockSpec((size, held, dim), lambda b, s: (jnp.minimum(b, steps - 2), 0, 0)),
                pl.BlockSpec((size, held, dim), lambda b, s: (0, 0, 0)),
                low_spec,
            ]
            + [blocks_of(size, rank, width)] * n
            + [pl.BlockSpec(memory_space=pl.ANY)],
            out_specs=blocks_of(size, held, dim),
        ),
        input_output_aliases={4 + n: 0},
        compiler_params=params(),
        cost_estimate=tiny_cost(),
    )(me, carrier, early, with_low, *pieces, result)


def place_blocks(block, first, result, shape):
    count, held = block.shape[:2]
    into = [] if result is None else [result]
    return pl.pallas_call(
        functools.partial(place_kernel, first, count),
        out_shape=jax.ShapeDtypeStruct(shape, jnp.bfloat16),
        in_specs=[pl.BlockSpec(memory_space=pltpu.VMEM)]
        + [pl.BlockSpec(memory_space=pl.ANY)] * len(into),
        out_specs=pl.BlockSpec(memory_space=pl.ANY),
        scratch_shapes=[pltpu.SemaphoreType.DMA],
        input_output_aliases={1: 0} if into else {},
        compiler_params=params(4),
        cost_estimate=tiny_cost(),
    )(block, *into)


def norm_rows(block_rows, gain):
    values = block_rows.astype(jnp.float32)
    scale = lax.rsqrt(jnp.mean(values * values, axis=-1, keepdims=True) + 1e-05)
    return (values * scale * gain.astype(jnp.float32)).astype(jnp.bfloat16)


def apply_adapter(block_rows, gain, down_maps, up_maps):
    values = block_rows.astype(jnp.float32)
    normed = norm_rows(block_rows, gain)
    low = jnp.einsum("bnd,brd->bnr", normed, down_maps, preferred_element_type=jnp.float32).astype(
        jnp.bfloat16
    )
    update = jnp.einsum("bnr,brd->bnd", low, up_maps, preferred_element_type=jnp.float32)
    return (values + update).astype(jnp.bfloat16)


def gathered_whole(
    activations, block_expert, seq_task, norm_gain, task_embed, expert_embed, gen_down, gen_up
):
    rows = activations[0]
    expert_ids = block_expert[0, :, 0]
    n_blocks = expert_ids.shape[0]
    per_seq = n_blocks // seq_task.shape[1]
    task_ids = seq_task[0][jnp.arange(n_blocks, dtype=jnp.int32) // per_seq]
    code_all = jax.nn.silu(
        task_embed.astype(jnp.float32)[:, None, :] + expert_embed[0].astype(jnp.float32)[None]
    ).astype(jnp.bfloat16)
    code_rows = code_all[task_ids, expert_ids]
    down_part = jnp.einsum(
        "bh,hrd->brd", code_rows, gen_down[0], preferred_element_type=jnp.float32
    ).astype(jnp.bfloat16)
    up_part = jnp.einsum(
        "bh,hrd->brd", code_rows, gen_up[0], preferred_element_type=jnp.float32
    ).astype(jnp.bfloat16)
    down_full, up_full = (
        lax.all_gather(down_part, "expert", axis=2, tiled=True),
        lax.all_gather(up_part, "expert", axis=2, tiled=True),
    )
    result = apply_adapter(rows, norm_gain[0], down_full, up_full)
    return passed_along(result[None], "section", 1)


def on_device(
    activations, block_expert, seq_task, norm_gain, task_embed, expert_embed, gen_down, gen_up
):
    n_blocks, held, dim = activations.shape[1:]
    rank, width = gen_down.shape[2:]
    n_devices = lax.axis_size("expert")
    raw, early = n_blocks // 2, n_blocks // 8
    chunks = [(raw, raw + n_blocks // 4), (raw + n_blocks // 4, n_blocks)]
    aligned = held % 16 == 0 and rank % 16 == 0 and width % LANES == 0
    if not aligned or n_blocks % 32 or raw % n_devices or n_devices % CORES or n_devices // CORES != 4:
        return gathered_whole(
            activations, block_expert, seq_task, norm_gain, task_embed, expert_embed, gen_down, gen_up
        )

    rows = activations[0]
    carried = raw - early
    early_sent = passed_along(rows[carried:raw], "section", 1)
    whole, raw_down, carrier, *chunk_maps = generated(
        block_expert[0, :, 0], seq_task[0], task_embed, expert_embed, gen_down, gen_up,
        rows, raw, carried, chunks,
    )
    carrier_sent = passed_along(carrier, "section", 1)
    ups = carrier_sent[carried:].reshape(-1, held, n_devices, width).swapaxes(1, 2)
    me = jnp.reshape(lax.axis_index("expert"), (1,)).astype(jnp.int32)
    other = core_swap(whole)

    ends, swaps = [], []

    class Gather:
        def __init__(self, block):
            self.held, self.pieces = block, [block]

        def step(self, *after, before_swap=(), split=False):
            k = len(ends)
            after = [*after, *ends[max(k - 2, 0) : max(k - 1, 0)], *swaps[max(k - 3, 0) : max(k - 2, 0)]]
            ends.append(ring_step(tied(self.held, *after) if after else self.held))
            if split:
                self.pieces += [ends[-1], [core_swap(half) for half in ends[-1]]]
                swaps.append(self.pieces[-1][0])
                return
            swaps.append(core_swap(tied(ends[-1], *before_swap) if before_swap else ends[-1]))
            self.held = ends[-1]
            self.pieces += [ends[-1], swaps[-1]]

    first, second = (Gather(block) for block in chunk_maps)
    downs, ups = Gather(raw_down), Gather(ups.reshape(raw, rank, width))
    (at, end), (middle, last) = chunks[0], (chunks[1][0] + n_blocks // 8, n_blocks)
    result = None
    first.step()
    first.step()
    downs.step(early_sent)
    first.step()
    first_out = layer_blocks(me, rows, at, end - at, norm_gain, other, first.pieces, first.pieces, 0)
    first_sent = passed_along(tied(first_out, early_sent), "section", 1)
    second.step()
    downs.step()
    downs.step(first_out)
    low = low_blocks(me, rows, norm_gain, other, downs.pieces)
    second.step(before_swap=[low])
    second.step(split=True)
    maps = second.pieces[:-1] + second.pieces[-1][:1], second.pieces[:-1] + second.pieces[-1][1:]
    second_out = layer_blocks(me, rows, end, middle - end, norm_gain, other, *maps, 0, low)
    second_sent = passed_along(tied(second_out, carrier_sent), "section", 1)
    third_out = layer_blocks(me, rows, middle, last - middle, norm_gain, other, *maps, middle - end)
    third_sent = passed_along(tied(third_out, first_sent), "section", 1)
    ups.step()
    ups.step(second_out)
    result = place_blocks(first_sent, at, None, rows.shape)
    ups.held, result = lax.optimization_barrier((ups.held, result))
    ups.step(third_out)

    maps = [ups.pieces[0], core_swap(ups.pieces[0])] + ups.pieces[1:]
    result = place_blocks(second_sent, end, result, rows.shape)
    result = update_blocks(me, carrier_sent, early_sent, second_sent, maps, result)
    return place_blocks(third_sent, middle, result, rows.shape)[None]


def solution(mesh):
    in_specs = (
        P("section", "groups", "expert", None),
        P("section", "groups", None),
        P("section", "groups"),
        P("section", None),
        P(),
        P("section", None, None),
        P("section", None, None, "expert"),
        P("section", None, None, "expert"),
    )
    out_specs = P("section", "groups", "expert", None)
    return jax.shard_map(
        on_device, mesh=mesh, in_specs=in_specs, out_specs=out_specs, check_vma=False
    )
```
